32 devices in a mesh: pp: 4 (over x, core), ep: 8 (over z, y).
Axes of the slice: x: 2, y: 2, z: 4, core: 2. Of those that a mesh axis runs over, the one named last changes fastest.
Arguments:
- x_fwd: bfloat16 [4, 512, 7168], P('pp', 'ep'), may hold values from -6 to 6
- dy_bwd: bfloat16 [4, 512, 7168], P('pp', 'ep'), may hold values from -6 to 6
- routes_fwd: int32 [4, 512, 8], P('pp', 'ep'), may hold values from 0 to 255, as said below
- routes_bwd: int32 [4, 512, 8], P('pp', 'ep'), may hold values from 0 to 255, as said below
- score_fwd: float32 [4, 512, 8], P('pp', 'ep'), may hold values from 0.05 to 1
- score_bwd: float32 [4, 512, 8], P('pp', 'ep'), may hold values from 0.05 to 1
- saved_bwd: float32 [4, 8, 2, 2, 1024], P('pp', None, None, None, 'ep'), may hold values from -6 to 6
- w_gate: bfloat16 [7168, 1024], P(None, 'ep'), may hold values from -0.0625 to 0.0625
- w_up: bfloat16 [7168, 1024], P(None, 'ep'), may hold values from -0.0625 to 0.0625
- w_down: bfloat16 [1024, 7168], P('ep'), may hold values from -0.1875 to 0.1875
Outputs:
- received: bfloat16 [4, 512, 7168], P('pp', 'ep')
The draws below stay inside these ranges and needn't reach their ends.
Inputs may be any that keep to these rules, and one draw needn't show every extreme that they name: `routes_fwd`: each token names 8 different ids. Within the 64 tokens of one block of a section, each expert below 1 is named at most 2 times, and in every section some expert below 1 is named exactly 2 times in every block. `routes_bwd`: the same as for routes_fwd.
All inputs are finite; a program needn't handle non-finite values.
Results may differ from the reference program's by a relative error of at most 0.008.
Values may be sent and summed in bfloat16 or wider, within the bound.
A program may use at most 64 MiB of HBM per device.

```python
import math
import jax
import jax.numpy as jnp
from jax import lax

D = 7168
EXPERTS = 256
TOPK = 8
HID_DEV = 128
SPLIT = 8
CAP = 2
TOK_DEV = 64
HID = 1024
EXP_SECTION = 1
SECTIONS = 4
TOKENS = 512
N_EP = 8


def route_draw(key, salt):
    key = jax.random.fold_in(key, salt)
    keys = jax.random.split(key, 5)
    blocks = TOKENS // TOK_DEV
    total_tokens = SECTIONS * TOKENS
    hot_expert = jax.random.randint(keys[0], (SECTIONS, 1, 1), 0, EXP_SECTION)
    counts = jax.random.randint(keys[1], (SECTIONS, blocks, EXP_SECTION), 0, CAP + 1)
    expert_ids = jnp.arange(EXP_SECTION, dtype=jnp.int32)[None, None, :]
    counts = jnp.where(expert_ids == hot_expert, CAP, counts)
    token_scores = jax.random.randint(keys[2], (SECTIONS, blocks, EXP_SECTION, TOK_DEV), 0, 1 << 20) * TOK_DEV
    token_scores = token_scores + jnp.arange(TOK_DEV, dtype=jnp.int32)
    ranks = jnp.argsort(jnp.argsort(token_scores, axis=-1), axis=-1)
    flagged = (ranks < counts[..., None]).astype(jnp.int32)
    flagged = jnp.transpose(flagged, (0, 1, 3, 2)).reshape(total_tokens, EXP_SECTION)
    order_keys = (1 - flagged) * EXP_SECTION + jnp.arange(EXP_SECTION, dtype=jnp.int32)[None, :]
    window_ids = jnp.argsort(order_keys, axis=-1).astype(jnp.int32)
    window_count = jnp.sum(flagged, axis=-1)
    if TOPK > EXP_SECTION:
        window_ids = jnp.concatenate([window_ids, jnp.zeros((total_tokens, TOPK - EXP_SECTION), jnp.int32)], axis=1)
    perm_keys = jax.random.split(keys[3], total_tokens)
    others = jax.vmap(lambda one_key: jax.random.permutation(one_key, EXPERTS - EXP_SECTION)[:TOPK])(perm_keys)
    others = others.astype(jnp.int32) + EXP_SECTION
    positions = jnp.arange(TOPK, dtype=jnp.int32)[None, :]
    chosen = jnp.where(positions < window_count[:, None], window_ids[:, :TOPK], others)
    shuffle_scores = jax.random.randint(keys[4], (total_tokens, TOPK), 0, 1 << 20) * TOPK + positions
    shuffle_order = jnp.argsort(shuffle_scores, axis=-1)
    chosen = jnp.take_along_axis(chosen, shuffle_order, axis=-1)
    return chosen.reshape(SECTIONS, TOKENS, TOPK).astype(jnp.int32)


def draw_routes_fwd(key, part):
    return route_draw(key, 101)


def draw_routes_bwd(key, part):
    return route_draw(key, 202)


def levels(stream_key, dims, shards, low, largest):
    level = 1.0
    for axis_at, shards_of in shards:
        steps = jax.random.uniform(jax.random.fold_in(jax.random.fold_in(stream_key, 6), axis_at), (shards_of,), jnp.float32, low / len(shards), largest / len(shards))
        level = level * jnp.repeat(jnp.exp(steps), dims[axis_at] // shards_of).reshape((-1,) + (1,) * (len(dims) - 1 - axis_at))
    return level


def gaussian(own_key, extent, width, bound, cuts=(), kind=jnp.bfloat16):
    gain = levels(own_key, extent, cuts, -0.22, 0.18) if cuts else 1.0
    result = jax.random.normal(own_key, extent, jnp.float32) * width * gain
    return jnp.minimum(jnp.maximum(result, -bound), bound).astype(kind)


def setup_inputs(seed: int = 0) -> dict:
    streams_of = jax.random.split(jax.random.key(seed), 11)
    return {
        "x_fwd": gaussian(streams_of[0], (SECTIONS, TOKENS, D), 1.0, 6.0, ((0, 4), (1, 8))),
        "dy_bwd": gaussian(streams_of[1], (SECTIONS, TOKENS, D), 1.0, 6.0, ((0, 4), (1, 8))),
        "routes_fwd": draw_routes_fwd(jax.random.fold_in(streams_of[10], 71), 0),
        "routes_bwd": draw_routes_bwd(jax.random.fold_in(streams_of[10], 71), 0),
        "score_fwd": jnp.clip(jnp.exp(math.log(1.0) - 2.9957323 * jax.random.uniform(streams_of[4], (SECTIONS, TOKENS, TOPK), jnp.float32) ** levels(streams_of[4], (SECTIONS, TOKENS, TOPK), ((0, 4), (1, 8)), -0.2, 0.2)), 0.05, 1.0),
        "score_bwd": jnp.clip(jnp.exp(math.log(1.0) - 2.9957323 * jax.random.uniform(streams_of[5], (SECTIONS, TOKENS, TOPK), jnp.float32) ** levels(streams_of[5], (SECTIONS, TOKENS, TOPK), ((0, 4), (1, 8)), -0.2, 0.2)), 0.05, 1.0),
        "saved_bwd": gaussian(streams_of[6], (SECTIONS, N_EP, CAP, 2, EXP_SECTION * HID), 1.0, 6.0, ((0, 4), (4, 8)), jnp.float32),
        "w_gate": gaussian(streams_of[7], (D, EXP_SECTION * HID), D ** -0.5, 0.0625, ((1, 8),)),
        "w_up": gaussian(streams_of[8], (D, EXP_SECTION * HID), D ** -0.5, 0.0625, ((1, 8),)),
        "w_down": gaussian(streams_of[9], (EXP_SECTION * HID, D), HID ** -0.5, 0.1875, ((0, 8),)),
    }


def route_tables(routes, scores):
    experts = jnp.arange(EXP_SECTION, dtype=jnp.int32)
    match = (routes[..., None] == experts).astype(jnp.float32)
    weight = 2.5 * scores / jnp.sum(scores, axis=-1, keepdims=True)
    hits = jnp.sum(match, axis=2)
    shares = jnp.sum(match * weight[..., None], axis=2)
    before = jnp.cumsum(hits, axis=1) - hits
    slots = jnp.arange(CAP, dtype=jnp.float32)
    placed = hits[..., None] * (before[..., None] == slots).astype(jnp.float32)
    return placed, placed * shares[..., None]


def gather_slots(placed, values):
    return jnp.einsum('btgc,btd->gbcd', placed, values.astype(jnp.float32)).astype(jnp.bfloat16)


def combine_slots(weighted, expert_out):
    return jnp.einsum('btgc,gbcd->btd', weighted, expert_out, precision=lax.Precision.HIGHEST)


def reference(x_fwd, dy_bwd, routes_fwd, routes_bwd, score_fwd, score_bwd, saved_bwd, w_gate, w_up, w_down):
    contract = (((1,), (1,)), ((), ()))

    def forward_expert(inputs):
        token_rows, expert = inputs
        flat_rows = token_rows.reshape(-1, D)
        first_col = (expert * HID).astype(jnp.int32)
        gate_cols = lax.dynamic_slice_in_dim(w_gate, first_col, HID, 1)
        up_cols = lax.dynamic_slice_in_dim(w_up, first_col, HID, 1)
        down_rows = lax.dynamic_slice_in_dim(w_down, first_col, HID, 0)
        gate_pre = jnp.dot(flat_rows, gate_cols, preferred_element_type=jnp.float32)
        up_pre = jnp.dot(flat_rows, up_cols, preferred_element_type=jnp.float32)
        hidden = (jax.nn.silu(gate_pre) * up_pre).astype(jnp.bfloat16)
        summed = jnp.zeros((flat_rows.shape[0], D), jnp.float32)
        for split_index in range(SPLIT):
            lower = split_index * HID_DEV
            partial_value = jnp.dot(hidden[:, lower:lower + HID_DEV], down_rows[lower:lower + HID_DEV],
                              preferred_element_type=jnp.float32)
            rounded = lax.optimization_barrier(partial_value.astype(jnp.bfloat16))
            summed = summed + rounded.astype(jnp.float32)
        return summed.reshape(token_rows.shape[0], token_rows.shape[1], D)

    def one_section(inputs):
        x_section, dy_section, routes_a, routes_b, score_a, score_b, saved_section = inputs
        experts = jnp.arange(EXP_SECTION, dtype=jnp.int32)

        def backward_expert(inner):
            token_rows, expert = inner
            flat_rows = token_rows.reshape(-1, D)
            first_col = (expert * HID).astype(jnp.int32)
            gate_cols = lax.dynamic_slice_in_dim(w_gate, first_col, HID, 1)
            up_cols = lax.dynamic_slice_in_dim(w_up, first_col, HID, 1)
            down_rows = lax.dynamic_slice_in_dim(w_down, first_col, HID, 0)
            gate_saved = lax.dynamic_slice_in_dim(saved_section[:, :, 0], first_col, HID, 2).reshape(-1, HID)
            up_saved = lax.dynamic_slice_in_dim(saved_section[:, :, 1], first_col, HID, 2).reshape(-1, HID)
            grad_hidden = lax.dot_general(flat_rows, down_rows, contract, preferred_element_type=jnp.float32)
            sigma = jax.nn.sigmoid(gate_saved)
            grad_gate = (grad_hidden * up_saved * sigma * (1.0 + gate_saved * (1.0 - sigma))).astype(jnp.bfloat16)
            grad_up = (grad_hidden * gate_saved * sigma).astype(jnp.bfloat16)
            summed = jnp.zeros((flat_rows.shape[0], D), jnp.float32)
            for split_index in range(SPLIT):
                lower = split_index * HID_DEV
                upper = lower + HID_DEV
                partial_value = lax.dot_general(grad_gate[:, lower:upper], gate_cols[:, lower:upper], contract,
                                          preferred_element_type=jnp.float32)
                partial_value = partial_value + lax.dot_general(grad_up[:, lower:upper], up_cols[:, lower:upper], contract,
                                                    preferred_element_type=jnp.float32)
                rounded = lax.optimization_barrier(partial_value.astype(jnp.bfloat16))
                summed = summed + rounded.astype(jnp.float32)
            return summed.reshape(token_rows.shape[0], token_rows.shape[1], D)

        placed_f, weighted_f = route_tables(routes_a.reshape(N_EP, TOK_DEV, TOPK), score_a.reshape(N_EP, TOK_DEV, TOPK))
        rows_f = gather_slots(placed_f, x_section.reshape(N_EP, TOK_DEV, D))
        out_f = lax.map(forward_expert, (rows_f, experts))
        routed_f = combine_slots(weighted_f, out_f).reshape(TOKENS, D).astype(jnp.bfloat16)
        placed_b, weighted_b = route_tables(routes_b.reshape(N_EP, TOK_DEV, TOPK), score_b.reshape(N_EP, TOK_DEV, TOPK))
        rows_b = gather_slots(placed_b, dy_section.reshape(N_EP, TOK_DEV, D))
        out_b = lax.map(backward_expert, (rows_b, experts))
        routed_b = combine_slots(weighted_b, out_b).reshape(TOKENS, D).astype(jnp.bfloat16)
        return routed_f, routed_b

    routed_f, routed_b = lax.map(one_section, (x_fwd, dy_bwd, routes_fwd, routes_bwd, score_fwd, score_bwd, saved_bwd))
    total = jnp.roll(routed_f, 1, axis=0).astype(jnp.float32) + jnp.roll(routed_b, -1, axis=0).astype(jnp.float32)
    return total.astype(jnp.bfloat16)
```

```python
import functools

import jax
import jax.numpy as jnp
from jax import lax
from jax.experimental import pallas as pl
from jax.experimental.pallas import tpu as pltpu
from jax.sharding import PartitionSpec as P

SPLIT = 8
CAP = 2
SUB = 8
PAIR = 2
MESH = pl.DeviceIdType.MESH
BF = jnp.bfloat16
F32 = jnp.float32
NT = (((1,), (1,)), ((), ()))
TN = (((0,), (0,)), ((), ()))


def each(count, step):
    if count <= 4:
        for at in range(count):
            step(at)
    else:
        lax.fori_loop(0, count, lambda at, carry: (step(at), carry)[1], 0)


def route_tables(routes, scores, groups):
    tokens, topk = routes.shape
    weight = 2.5 * scores / jnp.sum(scores, axis=-1, keepdims=True)
    earlier = lax.broadcasted_iota(jnp.int32, (tokens, tokens), 0)
    later = lax.broadcasted_iota(jnp.int32, (tokens, tokens), 1)
    order = (earlier < later).astype(F32)
    ones = jnp.ones((CAP * SUB, topk), F32)
    slot = lax.broadcasted_iota(jnp.int32, (CAP * SUB, tokens), 0) // SUB
    placed, weighted = [], []
    for group in range(groups):
        match = (routes == group).astype(F32)
        hits = lax.dot_general(ones, match, NT, preferred_element_type=F32)
        shares = lax.dot_general(
            ones, match * weight, NT, precision=lax.Precision.HIGHEST, preferred_element_type=F32
        )
        before = jnp.dot(hits, order, preferred_element_type=F32)
        here = hits * (before == slot.astype(F32)).astype(F32)
        placed.append(here)
        weighted.append(here * shares)
    return placed, weighted


def sub_mask(rows, lanes, part):
    return lax.broadcasted_iota(jnp.int32, (rows, lanes), 0) % SUB == part


def kernel(
    axes, groups,
    x_hbm, dy_hbm, rf_hbm, rb_hbm, sf_hbm, sb_hbm, saved_hbm, wg_hbm, wu_hbm, wd_hbm,
    total_ref, table_ref,
    x_s, dy_s, route_s, score_s, saved_s, wgu_s, wd_s,
    slots, rows, hid, grad, away, mine, pair_in, pair_out, final_in, table_s,
    load_sem, z_send, z_recv, y_send, y_recv, a_send, a_recv, f_send, f_recv, t_send, t_recv,
):
    sections, ep = axes
    high = ep // PAIR
    per_group = SPLIT // PAIR
    width = slots.shape[-1]
    hidden = wd_s.shape[1]
    p = lax.axis_index("pp")
    e = lax.axis_index("ep")
    hi, lo = e // PAIR, lax.rem(e, PAIR)
    other = 1 - lo
    after, before = lax.rem(p + 1, sections), lax.rem(p + sections - 1, sections)
    ahead = (after, before)

    loads = [
        pltpu.make_async_copy(rf_hbm, route_s.at[0], load_sem.at[0]),
        pltpu.make_async_copy(rb_hbm, route_s.at[1], load_sem.at[1]),
        pltpu.make_async_copy(sf_hbm, score_s.at[0], load_sem.at[2]),
        pltpu.make_async_copy(sb_hbm, score_s.at[1], load_sem.at[3]),
        pltpu.make_async_copy(x_hbm, x_s, load_sem.at[4]),
        pltpu.make_async_copy(dy_hbm, dy_s, load_sem.at[5]),
        pltpu.make_async_copy(saved_hbm, saved_s, load_sem.at[6]),
        pltpu.make_async_copy(wg_hbm, wgu_s.at[:, pl.ds(0, hidden)], load_sem.at[7]),
        pltpu.make_async_copy(wu_hbm, wgu_s.at[:, pl.ds(hidden, hidden)], load_sem.at[8]),
    ] + [
        pltpu.make_async_copy(wd_hbm.at[:, pl.ds(part * width, width)], wd_s.at[part], load_sem.at[9 + part])
        for part in range(SUB)
    ]
    for load in loads:
        load.start()

    barrier = pltpu.get_barrier_semaphore()

    def greet(section, at):
        pl.semaphore_signal(barrier, inc=1, device_id=(section, at), device_id_type=MESH)

    greet(p, hi * PAIR + other)
    each(high - 1, lambda k: greet(p, lax.rem(hi + k + 1, high) * PAIR + lo))
    each(high, lambda k: greet(after, lax.rem(hi + k, high) * PAIR + lo))
    each(high, lambda k: greet(before, lax.rem(hi + k, high) * PAIR + lo))

    for load in loads[:4]:
        load.wait()
    tables = [route_tables(route_s[d], score_s[d], groups) for d in range(2)]
    for d in range(2):
        for group in range(groups):
            table_s[d, pl.ds(group * CAP * SUB, CAP * SUB), :] = tables[d][1][group]

    def z_copy(d, k):
        to = lax.rem(hi + k, high)
        return pltpu.make_async_remote_copy(
            slots.at[d, to // per_group], rows.at[d, hi, lo],
            z_send.at[d, k], z_recv.at[d, k], (p, to * PAIR + lo), MESH,
        )

    def y_copy(d, k):
        block = lax.rem(hi + high - k, high)
        return pltpu.make_async_remote_copy(
            rows.at[d, block, lo], rows.at[d, block, lo],
            y_send.at[d, k], y_recv.at[d, k], (p, hi * PAIR + other), MESH,
        )

    def t_copy(d):
        return pltpu.make_async_remote_copy(
            table_s.at[d], table_ref.at[d], t_send.at[d], t_recv.at[d], (ahead[d], e), MESH
        )

    def pick(d):
        tokens = (x_s, dy_s)[d]
        loads[4 + d].wait()
        for group in range(groups):
            acc = jnp.zeros((CAP * SUB, width), F32)
            placed = tables[d][0][group]
            for part in range(SUB):
                chosen = jnp.where(sub_mask(CAP * SUB, placed.shape[1], part), placed, 0.0).astype(BF)
                acc += jnp.dot(
                    chosen, tokens[:, part * width:(part + 1) * width], preferred_element_type=F32
                )
            slots[d, group] = acc.astype(BF)
        rows[d, hi, lo] = slots[d, hi // per_group]

    pick(0)
    pl.semaphore_wait(barrier, PAIR - 1 + 3 * high - 1)
    for d in range(2):
        if d:
            pick(d)
        each(high - 1, lambda k, d=d: z_copy(d, k + 1).start())
        y_copy(d, 0).start()
    for d in range(2):
        t_copy(d).start()

    def relay(d):
        def step(k):
            z_copy(d, k + 1).wait_recv()
            y_copy(d, k + 1).start()
        each(high - 1, step)

    def gathered(d):
        each(high, lambda k: y_copy_in(d, k).wait_recv())

    def y_copy_in(d, k):
        block = lax.rem(hi + high - k, high)
        return pltpu.make_async_remote_copy(
            rows.at[d, block, other], rows.at[d, block, other],
            y_send.at[d, k], y_recv.at[d, k], (p, hi * PAIR + other), MESH,
        )

    relay(0)
    relay(1)

    block_rows = CAP * SUB
    step_high = min(high, 4)
    chunks = high // step_high
    full = step_high * PAIR * block_rows
    half = step_high * block_rows

    def spread(value):
        count, lanes = value.shape
        summed = jnp.sum(value.reshape(count // SUB, SUB, lanes), axis=1, keepdims=True)
        return jnp.broadcast_to(summed, (count // SUB, SUB, lanes)).reshape(count, lanes)

    def at_chunk(chunk):
        return pl.ds(chunk * step_high, step_high)

    def forward_hidden(chunk):
        held = rows[0, at_chunk(chunk)].reshape(full, width)
        acc = jnp.zeros((full, 2 * hidden), F32)
        for part in range(SUB):
            acc += jnp.dot(
                jnp.where(sub_mask(full, width, part), held, jnp.zeros_like(held)),
                wgu_s[pl.ds(part * width, width), :], preferred_element_type=F32,
            )
        pre = spread(acc)
        gate, up = pre[:, :hidden], pre[:, hidden:]
        value = (gate / (1.0 + jnp.exp(-gate)) * up).astype(BF)
        hid[at_chunk(chunk)] = value.reshape(step_high, PAIR, block_rows, hidden)

    def backward_hidden(chunk):
        held = rows[1, at_chunk(chunk)].reshape(full, width)
        acc = jnp.zeros((full, hidden), F32)
        for part in range(SUB):
            acc += lax.dot_general(
                jnp.where(sub_mask(full, width, part), held, jnp.zeros_like(held)),
                wd_s[part], NT, preferred_element_type=F32,
            )
        grad_hidden = spread(acc)
        count = step_high * PAIR * CAP
        kept = saved_s[pl.ds(chunk * count, count)]
        gate = jnp.broadcast_to(kept[:, 0:1, :], (count, SUB, hidden)).reshape(full, hidden)
        up = jnp.broadcast_to(kept[:, 1:2, :], (count, SUB, hidden)).reshape(full, hidden)
        sigma = 1.0 / (1.0 + jnp.exp(-gate))
        grad_gate = (grad_hidden * up * sigma * (1.0 + gate * (1.0 - sigma))).astype(BF)
        grad_up = (grad_hidden * gate * sigma).astype(BF)
        both = jnp.concatenate([grad_gate, grad_up], axis=1)
        grad[at_chunk(chunk)] = both.reshape(step_high, PAIR, block_rows, 2 * hidden)

    def forward_out(chunk, side):
        held = hid[at_chunk(chunk), side].reshape(half, hidden)
        parts = [
            jnp.where(sub_mask(half, hidden, part), held, jnp.zeros_like(held)) for part in range(SUB)
        ]
        return jnp.dot(
            jnp.concatenate(parts, axis=1), wd_s[...].reshape(SUB * hidden, width),
            preferred_element_type=F32,
        )

    def backward_out(chunk, side):
        held = grad[at_chunk(chunk), side].reshape(half, 2 * hidden)
        acc = jnp.zeros((half, width), F32)
        for part in range(SUB):
            acc += lax.dot_general(
                jnp.where(sub_mask(half, 2 * hidden, part), held, jnp.zeros_like(held)),
                wgu_s[pl.ds(part * width, width), :], NT, preferred_element_type=F32,
            )
        return acc

    outs = (forward_out, backward_out)

    def a_copy(d, k):
        block = lax.rem(hi + k, high)
        return pltpu.make_async_remote_copy(
            away.at[d, block], pair_in.at[d, block],
            a_send.at[d, k], a_recv.at[d, k], (p, hi * PAIR + other), MESH,
        )

    def f_copy(d, k):
        block = lax.rem(hi + k, high)
        return pltpu.make_async_remote_copy(
            pair_out.at[d, block], final_in.at[d, hi],
            f_send.at[d, k], f_recv.at[d, k], (ahead[d], block * PAIR + lo), MESH,
        )

    def f_copy_in(d, k):
        block = lax.rem(hi + high - k, high)
        return pltpu.make_async_remote_copy(
            pair_out.at[d, block], final_in.at[d, block],
            f_send.at[d, k], f_recv.at[d, k], (ahead[d], block * PAIR + lo), MESH,
        )

    def partial(d):
        def out_away(chunk):
            away[d, at_chunk(chunk)] = outs[d](chunk, other).astype(BF).reshape(step_high, block_rows, width)
        each(chunks, out_away)
        each(high, lambda k: a_copy(d, k).start())

        def out_mine(chunk):
            mine[d, at_chunk(chunk)] = outs[d](chunk, lo).reshape(step_high, block_rows, width)
        each(chunks, out_mine)

    def pass_on(d):
        def step(k):
            block = lax.rem(hi + k, high)
            a_copy(d, k).wait_recv()
            pair_out[d, block] = (mine[d, block] + pair_in[d, block].astype(F32)).astype(BF)
            f_copy(d, k).start()
        each(high, step)

    for load in loads[6:]:
        load.wait()
    gathered(0)
    each(chunks, forward_hidden)
    partial(0)
    gathered(1)
    each(chunks, backward_hidden)
    pass_on(0)
    partial(1)
    pass_on(1)

    for d in range(2):
        each(high, lambda k, d=d: f_copy_in(d, k).wait_recv())
        for group in range(groups):
            acc = final_in[d, group * per_group].astype(F32)
            for at in range(1, per_group):
                acc += final_in[d, group * per_group + at].astype(F32)
            total_ref[d, pl.ds(group * block_rows, block_rows), :] = acc
        t_copy(d).wait_recv()

    for d in range(2):
        t_copy(d).wait_send()
        each(high - 1, lambda k, d=d: z_copy(d, k + 1).wait_send())
        each(high, lambda k, d=d: y_copy(d, k).wait_send())
        each(high, lambda k, d=d: a_copy(d, k).wait_send())
        each(high, lambda k, d=d: f_copy(d, k).wait_send())


def combine_kernel(groups, total_ref, table_ref, out_ref, column_s):
    part = pl.program_id(0)
    count = table_ref.shape[1]

    @pl.when(part == 0)
    def _():
        row = lax.broadcasted_iota(jnp.int32, (count, count), 0)
        col = lax.broadcasted_iota(jnp.int32, (count, count), 1)
        same = (row == col).astype(F32)
        for d in range(2):
            column_s[d] = lax.dot_general(
                table_ref[d], same, TN, precision=lax.Precision.HIGHEST, preferred_element_type=F32
            )

    routed = []
    for d in range(2):
        acc = None
        for slot in range(groups * CAP):
            term = column_s[d, :, slot * SUB:slot * SUB + 1] * total_ref[d, pl.ds(slot * SUB + part, 1), :]
            acc = term if acc is None else acc + term
        routed.append(acc.astype(BF).astype(F32))
    out_ref[0] = (routed[0] + routed[1]).astype(BF)


def solution(mesh):
    sections, ep = mesh.shape["pp"], mesh.shape["ep"]
    groups = ep // SPLIT
    high = ep // PAIR

    def body(x, dy, rf, rb, sf, sb, saved, wg, wu, wd):
        _, tokens, model = x.shape
        topk = rf.shape[2]
        hidden = wg.shape[1]
        width = model // SUB
        block_rows = CAP * SUB
        anywhere = pl.BlockSpec(memory_space=pl.ANY)
        vmem = pl.BlockSpec(memory_space=pltpu.VMEM)
        total, table = pl.pallas_call(
            functools.partial(kernel, (sections, ep), groups),
            out_shape=(
                jax.ShapeDtypeStruct((2, groups * block_rows, width), F32),
                jax.ShapeDtypeStruct((2, groups * block_rows, tokens), F32),
            ),
            in_specs=[anywhere] * 10,
            out_specs=(vmem, vmem),
            scratch_shapes=[
                pltpu.VMEM((tokens, model), BF),
                pltpu.VMEM((tokens, model), BF),
                pltpu.VMEM((2, tokens, topk), jnp.int32),
                pltpu.VMEM((2, tokens, topk), F32),
                pltpu.VMEM((ep * CAP, 2, hidden), F32),
                pltpu.VMEM((model, 2 * hidden), BF),
                pltpu.VMEM((SUB, hidden, width), BF),
                pltpu.VMEM((2, groups, block_rows, width), BF),
                pltpu.VMEM((2, high, PAIR, block_rows, width), BF),
                pltpu.VMEM((high, PAIR, block_rows, hidden), BF),
                pltpu.VMEM((high, PAIR, block_rows, 2 * hidden), BF),
                pltpu.VMEM((2, high, block_rows, width), BF),
                pltpu.VMEM((2, high, block_rows, width), F32),
                pltpu.VMEM((2, high, block_rows, width), BF),
                pltpu.VMEM((2, high, block_rows, width), BF),
                pltpu.VMEM((2, high, block_rows, width), BF),
                pltpu.VMEM((2, groups * block_rows, tokens), F32),
                pltpu.SemaphoreType.DMA((9 + SUB,)),
            ] + [pltpu.SemaphoreType.DMA((2, high))] * 8 + [pltpu.SemaphoreType.DMA((2,))] * 2,
            compiler_params=pltpu.CompilerParams(
                collective_id=0, has_side_effects=True, vmem_limit_bytes=48 * 1024 * 1024
            ),
            name="experts",
        )(x[0], dy[0], rf[0], rb[0], sf[0], sb[0], saved.reshape(ep * CAP, 2, hidden), wg, wu, wd)
        return pl.pallas_call(
            functools.partial(combine_kernel, groups),
            grid=(SUB,),
            out_shape=jax.ShapeDtypeStruct((1, tokens, model), BF),
            in_specs=[
                pl.BlockSpec(total.shape, lambda part: (0, 0, 0)),
                pl.BlockSpec(table.shape, lambda part: (0, 0, 0)),
            ],
            out_specs=pl.BlockSpec((1, tokens, width), lambda part: (0, 0, part)),
            scratch_shapes=[pltpu.VMEM((2, tokens, groups * block_rows), F32)],
            name="combine",
        )(total, table)

    in_specs = (
        P("pp", "ep", None),
        P("pp", "ep", None),
        P("pp", "ep", None),
        P("pp", "ep", None),
        P("pp", "ep", None),
        P("pp", "ep", None),
        P("pp", None, None, None, "ep"),
        P(None, "ep"),
        P(None, "ep"),
        P("ep", None),
    )
    out_specs = P("pp", "ep", None)
    return jax.shard_map(body, mesh=mesh, in_specs=in_specs, out_specs=out_specs, check_vma=False)
```

```python
import functools

import jax
import jax.numpy as jnp
from jax import lax
from jax.experimental import pallas as pl
from jax.experimental.pallas import tpu as pltpu
from jax.sharding import PartitionSpec as P

SPLIT = 8
CAP = 2
SUB = 8
PAIR = 2
VMEM_BYTES = 60 * 1024 * 1024
MESH = pl.DeviceIdType.MESH
BF = jnp.bfloat16
F32 = jnp.float32
NT = (((1,), (1,)), ((), ()))
TN = (((0,), (0,)), ((), ()))


def each(count, step):
    if count <= 4:
        for at in range(count):
            step(at)
    else:
        lax.fori_loop(0, count, lambda at, carry: (step(at), carry)[1], 0)


def route_tables(routes, scores, groups):
    tokens = routes.shape[1]
    weight = 2.5 * scores / jnp.sum(scores, axis=0, keepdims=True)
    earlier = lax.broadcasted_iota(jnp.int32, (tokens, tokens), 0)
    later = lax.broadcasted_iota(jnp.int32, (tokens, tokens), 1)
    order = (earlier < later).astype(F32)
    rows = CAP * SUB
    slot = (lax.broadcasted_iota(jnp.int32, (rows, tokens), 0) // SUB).astype(F32)
    placed, weighted = [], []
    for group in range(groups):
        match = (routes == group).astype(F32)
        hits = jnp.broadcast_to(jnp.sum(match, axis=0, keepdims=True), (rows, tokens))
        shares = jnp.broadcast_to(jnp.sum(match * weight, axis=0, keepdims=True), (rows, tokens))
        before = jnp.dot(hits, order, preferred_element_type=F32)
        here = hits * (before == slot).astype(F32)
        placed.append(here)
        weighted.append(here * shares)
    return placed, weighted


def masks(lanes):
    part = lax.broadcasted_iota(jnp.int32, (CAP * SUB, lanes), 0) & (SUB - 1)
    return [part == at for at in range(SUB)]


def masked(held, mask):
    blocks, rows, lanes = held.shape
    return jnp.where(mask[None], held, jnp.zeros_like(held)).reshape(blocks * rows, lanes)


def kernel(
    axes, groups, lane_chunks,
    x_hbm, dy_hbm, rf_hbm, rb_hbm, sf_hbm, sb_hbm, saved_hbm, wg_hbm, wu_hbm, wd_hbm,
    out_hbm,
    tokens_s, route_s, score_s, saved_s, wgu_s, wd_s,
    slots, rows, hid, grad, away, mine, pair_in, pair_out, final_in, table_s, table_in, routed_s, out_s,
    load_sem, out_sem, z_send, z_recv, y_send, y_recv, a_send, a_recv, f_send, f_recv, t_send, t_recv,
):
    sections, ep = axes
    high = ep // PAIR
    per_group = SPLIT // PAIR
    width = slots.shape[-1]
    count = x_hbm.shape[0]
    hidden = wd_s.shape[0] // SUB
    p = lax.axis_index("pp")
    e = lax.axis_index("ep")
    hi, lo = e // PAIR, lax.rem(e, PAIR)
    other = 1 - lo
    after, before = lax.rem(p + 1, sections), lax.rem(p + sections - 1, sections)
    ahead = (after, before)

    def columns(part):
        return pl.ds(part * width, width)

    small = [
        pltpu.make_async_copy(rf_hbm, route_s.at[0], load_sem.at[0]),
        pltpu.make_async_copy(rb_hbm, route_s.at[1], load_sem.at[1]),
        pltpu.make_async_copy(sf_hbm, score_s.at[0], load_sem.at[2]),
        pltpu.make_async_copy(sb_hbm, score_s.at[1], load_sem.at[3]),
    ]
    inputs = [
        [
            pltpu.make_async_copy(
                hbm.at[:, columns(part)], tokens_s.at[d, pl.ds(part * count, count)],
                load_sem.at[4 + d * SUB + part],
            )
            for part in range(SUB)
        ]
        for d, hbm in enumerate((x_hbm, dy_hbm))
    ]
    first = 4 + 2 * SUB
    saved_load = [pltpu.make_async_copy(saved_hbm, saved_s, load_sem.at[first + 3 * SUB])]
    up_loads = [
        pltpu.make_async_copy(
            hbm.at[columns(part), :],
            wgu_s.at[:, pl.ds((2 * part + side) * hidden, hidden)],
            load_sem.at[first + side * SUB + part],
        )
        for part in range(SUB)
        for side, hbm in enumerate((wg_hbm, wu_hbm))
    ]
    down_loads = [
        pltpu.make_async_copy(
            wd_hbm.at[:, columns(part)], wd_s.at[pl.ds(part * hidden, hidden)],
            load_sem.at[first + 2 * SUB + part],
        )
        for part in range(SUB)
    ]
    for load in small + inputs[0]:
        load.start()

    barrier = pltpu.get_barrier_semaphore()

    def greet(section, at):
        pl.semaphore_signal(barrier, inc=1, device_id=(section, at), device_id_type=MESH)

    greet(p, hi * PAIR + other)
    each(high - 1, lambda k: greet(p, lax.rem(hi + k + 1, high) * PAIR + lo))
    each(high, lambda k: greet(after, lax.rem(hi + k, high) * PAIR + lo))
    each(high, lambda k: greet(before, lax.rem(hi + k, high) * PAIR + lo))

    for load in inputs[1] + up_loads + down_loads + saved_load:
        load.start()

    for load in small:
        load.wait()
    tables = [route_tables(route_s[d], score_s[d], groups) for d in range(2)]
    block_rows = CAP * SUB
    for d in range(2):
        for group in range(groups):
            table_s[d, pl.ds(group * block_rows, block_rows), :] = tables[d][1][group]

    def z_copy(d, k):
        to = lax.rem(hi + k, high)
        return pltpu.make_async_remote_copy(
            slots.at[d, to // per_group], rows.at[d, hi, lo],
            z_send.at[d, k], z_recv.at[d, k], (p, to * PAIR + lo), MESH,
        )

    def y_copy(d, k, side):
        block = lax.rem(hi + high - k, high)
        return pltpu.make_async_remote_copy(
            rows.at[d, block, side], rows.at[d, block, side],
            y_send.at[d, k], y_recv.at[d, k], (p, hi * PAIR + other), MESH,
        )

    def t_copy(d):
        return pltpu.make_async_remote_copy(
            table_s.at[d], table_in.at[d], t_send.at[d], t_recv.at[d], (ahead[d], e), MESH
        )

    lanes = SUB * count
    own_part = lax.broadcasted_iota(jnp.int32, (block_rows, lanes), 0) & (SUB - 1)
    same_part = own_part == lax.broadcasted_iota(jnp.int32, (block_rows, lanes), 1) // count

    def pick(d):
        chosen = []
        for group in range(groups):
            wide = jnp.concatenate([tables[d][0][group]] * SUB, axis=1)
            chosen.append(jnp.where(same_part, wide, 0.0).astype(BF))
        for load in inputs[d]:
            load.wait()
        for group in range(groups):
            slots[d, group] = jnp.dot(
                chosen[group], tokens_s[d], preferred_element_type=F32
            ).astype(BF)
        rows[d, hi, lo] = slots[d, hi // per_group]

    pick(0)
    pl.semaphore_wait(barrier, PAIR - 1 + 3 * high - 1)
    for d in range(2):
        if d:
            pick(d)
        each(high - 1, lambda k, d=d: z_copy(d, k + 1).start())
        y_copy(d, 0, lo).start()
    for d in range(2):
        t_copy(d).start()

    def relay(d):
        def step(k):
            z_copy(d, k + 1).wait_recv()
            y_copy(d, k + 1, lo).start()
        each(high - 1, step)

    def gathered(d):
        each(high, lambda k: y_copy(d, k, other).wait_recv())

    step_high = min(high, 4)
    chunks = high // step_high
    blocks = step_high * PAIR
    full = blocks * block_rows
    half = step_high * block_rows

    def spread(value):
        size, wide = value.shape
        summed = jnp.sum(value.reshape(size // SUB, SUB, wide), axis=1, keepdims=True)
        return jnp.broadcast_to(summed, (size // SUB, SUB, wide)).reshape(size, wide)

    def at_chunk(chunk):
        return pl.ds(chunk * step_high, step_high)

    def forward_hidden(chunk):
        held = rows[0, at_chunk(chunk)].reshape(blocks, block_rows, width)
        acc = jnp.zeros((full, 2 * hidden), F32)
        for part, mask in enumerate(masks(width)):
            acc += jnp.dot(
                masked(held, mask), wgu_s[:, pl.ds(part * 2 * hidden, 2 * hidden)],
                preferred_element_type=F32,
            )
        pre = spread(acc)
        gate, up = pre[:, :hidden], pre[:, hidden:]
        value = (gate / (1.0 + jnp.exp(-gate)) * up).astype(BF)
        hid[at_chunk(chunk)] = value.reshape(step_high, PAIR, block_rows, hidden)

    def backward_hidden(chunk):
        held = rows[1, at_chunk(chunk)].reshape(blocks, block_rows, width)
        acc = jnp.zeros((full, hidden), F32)
        for part, mask in enumerate(masks(width)):
            acc += lax.dot_general(
                masked(held, mask), wd_s[pl.ds(part * hidden, hidden), :], NT,
                preferred_element_type=F32,
            )
        grad_hidden = spread(acc)
        size = step_high * PAIR * CAP
        kept = saved_s[pl.ds(chunk * size, size)]
        gate = jnp.broadcast_to(kept[:, 0:1, :], (size, SUB, hidden)).reshape(full, hidden)
        up = jnp.broadcast_to(kept[:, 1:2, :], (size, SUB, hidden)).reshape(full, hidden)
        sigma = 1.0 / (1.0 + jnp.exp(-gate))
        grad_gate = (grad_hidden * up * sigma * (1.0 + gate * (1.0 - sigma))).astype(BF)
        grad_up = (grad_hidden * gate * sigma).astype(BF)
        both = jnp.concatenate([grad_gate, grad_up], axis=1)
        grad[at_chunk(chunk)] = both.reshape(step_high, PAIR, block_rows, 2 * hidden)

    def side_parts(source, chunk):
        held = jnp.concatenate([source[at_chunk(chunk), other], source[at_chunk(chunk), lo]], axis=0)
        return jnp.concatenate([masked(held, mask) for mask in masks(held.shape[-1])], axis=1)

    def forward_out(chunk, cut):
        return jnp.dot(side_parts(hid, chunk), wd_s[:, cut], preferred_element_type=F32)

    def backward_out(chunk, cut):
        return lax.dot_general(side_parts(grad, chunk), wgu_s[cut, :], NT, preferred_element_type=F32)

    outs = (forward_out, backward_out)
    cuts = [pl.ds(low, size) for low, size in lane_chunks]

    def a_copy(d, n):
        return pltpu.make_async_remote_copy(
            away.at[d, :, :, cuts[n]], pair_in.at[d, :, :, cuts[n]],
            a_send.at[d, n], a_recv.at[d, n], (p, hi * PAIR + other), MESH,
        )

    def f_copy(d, n, k, arriving=False):
        block = lax.rem(hi + (high - k if arriving else k), high)
        slot = block if arriving else hi
        return pltpu.make_async_remote_copy(
            pair_out.at[d, block, :, cuts[n]], final_in.at[d, slot, :, cuts[n]],
            f_send.at[d, n, k], f_recv.at[d, n, k], (ahead[d], block * PAIR + lo), MESH,
        )

    def partial(d):
        for n, cut in enumerate(cuts):
            def make(chunk, cut=cut):
                value = outs[d](chunk, cut)
                shape = (step_high, block_rows, value.shape[1])
                away[d, at_chunk(chunk), :, cut] = value[:half].astype(BF).reshape(shape)
                mine[d, at_chunk(chunk), :, cut] = value[half:].reshape(shape)
            each(chunks, make)
            a_copy(d, n).start()

    def pass_on(d):
        for n, cut in enumerate(cuts):
            a_copy(d, n).wait_recv()

            def add(k, n=n, cut=cut):
                block = lax.rem(hi + k, high)
                pair_out[d, block, :, cut] = (
                    mine[d, block, :, cut] + pair_in[d, block, :, cut].astype(F32)
                ).astype(BF)
                f_copy(d, n, k).start()
            each(high, add)

    def route_columns(d):
        t_copy(d).wait_recv()
        size = table_in.shape[1]
        row = lax.broadcasted_iota(jnp.int32, (size, size), 0)
        col = lax.broadcasted_iota(jnp.int32, (size, size), 1)
        return lax.dot_general(
            table_in[d], (row == col).astype(F32), TN,
            precision=lax.Precision.HIGHEST, preferred_element_type=F32,
        )

    def finish(d, table):
        for n in range(len(cuts)):
            each(high, lambda k, n=n: f_copy(d, n, k, True).wait_recv())
        totals = []
        for group in range(groups):
            acc = final_in[d, group * per_group].astype(F32)
            for at in range(1, per_group):
                acc += final_in[d, group * per_group + at].astype(F32)
            totals.append(acc)
        for part in range(SUB):
            acc = None
            for group in range(groups):
                for slot in range(CAP):
                    at = slot * SUB + part
                    column = group * block_rows + slot * SUB
                    term = table[:, column:column + 1] * totals[group][at:at + 1, :]
                    acc = term if acc is None else acc + term
            routed = acc.astype(BF)
            if d == 0:
                routed_s[:, columns(part)] = routed
            else:
                out_s[:, columns(part)] = (
                    routed_s[:, columns(part)].astype(F32) + routed.astype(F32)
                ).astype(BF)
                out_copy(part).start()

    def out_copy(part):
        return pltpu.make_async_copy(
            out_s.at[:, columns(part)], out_hbm.at[:, columns(part)], out_sem.at[part]
        )

    relay(0)
    for load in up_loads:
        load.wait()
    gathered(0)
    each(chunks, forward_hidden)
    relay(1)
    for load in down_loads + saved_load:
        load.wait()
    partial(0)
    gathered(1)
    each(chunks, backward_hidden)
    pass_on(0)
    partial(1)
    table_f, table_b = route_columns(0), route_columns(1)
    pass_on(1)
    finish(0, table_f)
    finish(1, table_b)

    for d in range(2):
        t_copy(d).wait_send()
        each(high - 1, lambda k, d=d: z_copy(d, k + 1).wait_send())
        each(high, lambda k, d=d: y_copy(d, k, lo).wait_send())
        for n in range(len(cuts)):
            a_copy(d, n).wait_send()
            each(high, lambda k, d=d, n=n: f_copy(d, n, k).wait_send())
    for part in range(SUB):
        out_copy(part).wait()


def solution(mesh):
    sections, ep = mesh.shape["pp"], mesh.shape["ep"]
    groups = ep // SPLIT
    high = ep // PAIR

    def body(x, dy, rf, rb, sf, sb, saved, wg, wu, wd):
        _, tokens, model = x.shape
        topk = rf.shape[2]
        hidden = wg.shape[1]
        width = model // SUB
        block_rows = CAP * SUB
        early = width // 256 * 128 + 128 if width > 256 else width
        lane_chunks = [(0, early), (early, width - early)] if early < width else [(0, width)]
        cuts = len(lane_chunks)
        anywhere = pl.BlockSpec(memory_space=pl.ANY)
        out = pl.pallas_call(
            functools.partial(kernel, (sections, ep), groups, lane_chunks),
            out_shape=jax.ShapeDtypeStruct((tokens, model), BF),
            in_specs=[anywhere] * 10,
            out_specs=anywhere,
            scratch_shapes=[
                pltpu.VMEM((2, SUB * tokens, width), BF),
                pltpu.VMEM((2, topk, tokens), jnp.int32),
                pltpu.VMEM((2, topk, tokens), F32),
                pltpu.VMEM((ep * CAP, 2, hidden), F32),
                pltpu.VMEM((width, SUB * 2 * hidden), BF),
                pltpu.VMEM((SUB * hidden, width), BF),
                pltpu.VMEM((2, groups, block_rows, width), BF),
                pltpu.VMEM((2, high, PAIR, block_rows, width), BF),
                pltpu.VMEM((high, PAIR, block_rows, hidden), BF),
                pltpu.VMEM((high, PAIR, block_rows, 2 * hidden), BF),
                pltpu.VMEM((2, high, block_rows, width), BF),
                pltpu.VMEM((2, high, block_rows, width), F32),
                pltpu.VMEM((2, high, block_rows, width), BF),
                pltpu.VMEM((2, high, block_rows, width), BF),
                pltpu.VMEM((2, high, block_rows, width), BF),
                pltpu.VMEM((2, groups * block_rows, tokens), F32),
                pltpu.VMEM((2, groups * block_rows, tokens), F32),
                pltpu.VMEM((tokens, model), BF),
                pltpu.VMEM((tokens, model), BF),
                pltpu.SemaphoreType.DMA((5 + 5 * SUB,)),
                pltpu.SemaphoreType.DMA((SUB,)),
            ]
            + [pltpu.SemaphoreType.DMA((2, high))] * 4
            + [pltpu.SemaphoreType.DMA((2, cuts))] * 2
            + [pltpu.SemaphoreType.DMA((2, cuts, high))] * 2
            + [pltpu.SemaphoreType.DMA((2,))] * 2,
            compiler_params=pltpu.CompilerParams(
                collective_id=0, has_side_effects=True, vmem_limit_bytes=VMEM_BYTES
            ),
            name="experts",
        )(
            x[0], dy[0], rf[0].T, rb[0].T, sf[0].T, sb[0].T,
            saved.reshape(ep * CAP, 2, hidden), wg, wu, wd,
        )
        return out[None]

    in_specs = (
        P("pp", "ep", None),
        P("pp", "ep", None),
        P("pp", "ep", None),
        P("pp", "ep", None),
        P("pp", "ep", None),
        P("pp", "ep", None),
        P("pp", None, None, None, "ep"),
        P(None, "ep"),
        P(None, "ep"),
        P("ep", None),
    )
    out_specs = P("pp", "ep", None)
    return jax.shard_map(body, mesh=mesh, in_specs=in_specs, out_specs=out_specs, check_vma=False)
```

```python
import functools

import jax
import jax.numpy as jnp
from jax import lax
from jax.experimental import pallas as pl
from jax.experimental.pallas import tpu as pltpu
from jax.sharding import PartitionSpec as P

SPLIT = 8
CAP = 2
SUB = 8
PAIR = 2
VMEM_BYTES = 60 * 1024 * 1024
MESH = pl.DeviceIdType.MESH
BF = jnp.bfloat16
F32 = jnp.float32
NT = (((1,), (1,)), ((), ()))
TN = (((0,), (0,)), ((), ()))


def each(count, step):
    if count <= 4:
        for at in range(count):
            step(at)
    else:
        lax.fori_loop(0, count, lambda at, carry: (step(at), carry)[1], 0)


def route_tables(routes, scores, groups):
    tokens = routes.shape[1]
    weight = 2.5 * scores / jnp.sum(scores, axis=0, keepdims=True)
    earlier = lax.broadcasted_iota(jnp.int32, (tokens, tokens), 0)
    later = lax.broadcasted_iota(jnp.int32, (tokens, tokens), 1)
    order = (earlier < later).astype(F32)
    rows = CAP * SUB
    slot = (lax.broadcasted_iota(jnp.int32, (rows, tokens), 0) // SUB).astype(F32)
    placed, weighted = [], []
    for group in range(groups):
        match = (routes == group).astype(F32)
        hits = jnp.broadcast_to(jnp.sum(match, axis=0, keepdims=True), (rows, tokens))
        shares = jnp.broadcast_to(jnp.sum(match * weight, axis=0, keepdims=True), (rows, tokens))
        before = jnp.dot(hits, order, preferred_element_type=F32)
        here = hits * (before == slot).astype(F32)
        placed.append(here)
        weighted.append(here * shares)
    return placed, weighted


def masks(lanes):
    part = lax.broadcasted_iota(jnp.int32, (CAP * SUB, lanes), 0) & (SUB - 1)
    return [part == at for at in range(SUB)]


def masked(held, mask):
    blocks, rows, lanes = held.shape
    return jnp.where(mask[None], held, jnp.zeros_like(held)).reshape(blocks * rows, lanes)


def kernel(
    axes, groups, lane_chunks,
    x_hbm, dy_hbm, rf_hbm, rb_hbm, sf_hbm, sb_hbm, saved_hbm, wg_hbm, wu_hbm, wd_hbm,
    out_hbm,
    tokens_s, route_s, score_s, saved_s, wgu_s, wd_s,
    saved_in, slots, rows, hid, grad, parts_s, away, mine, pair_in, pair_out, final_in, table_s, table_in, routed_s, out_s,
    load_sem, out_sem, z_send, z_recv, y_send, y_recv, a_send, a_recv, f_send, f_recv, t_send, t_recv, s_send, s_recv,
):
    sections, ep = axes
    high = ep // PAIR
    per_group = SPLIT // PAIR
    width = slots.shape[-1]
    count = x_hbm.shape[0]
    hidden = wd_s.shape[0] // SUB
    p = lax.axis_index("pp")
    e = lax.axis_index("ep")
    hi, lo = e // PAIR, lax.rem(e, PAIR)
    other = 1 - lo
    after, before = lax.rem(p + 1, sections), lax.rem(p + sections - 1, sections)
    ahead = (after, before)
    works_for = (p, before)
    gives_to = (after, p)

    def columns(part):
        return pl.ds(part * width, width)

    small = [
        pltpu.make_async_copy(rf_hbm, route_s.at[0], load_sem.at[0]),
        pltpu.make_async_copy(rb_hbm, route_s.at[1], load_sem.at[1]),
        pltpu.make_async_copy(sf_hbm, score_s.at[0], load_sem.at[2]),
        pltpu.make_async_copy(sb_hbm, score_s.at[1], load_sem.at[3]),
    ]
    inputs = [
        [
            pltpu.make_async_copy(
                hbm.at[:, columns(part)], tokens_s.at[d, pl.ds(part * count, count)],
                load_sem.at[4 + d * SUB + part],
            )
            for part in range(SUB)
        ]
        for d, hbm in enumerate((x_hbm, dy_hbm))
    ]
    first = 4 + 2 * SUB
    saved_load = [pltpu.make_async_copy(saved_hbm, saved_s, load_sem.at[first + 3 * SUB])]
    up_loads = [
        pltpu.make_async_copy(
            hbm.at[columns(part), :],
            wgu_s.at[:, pl.ds((2 * part + side) * hidden, hidden)],
            load_sem.at[first + side * SUB + part],
        )
        for part in range(SUB)
        for side, hbm in enumerate((wg_hbm, wu_hbm))
    ]
    down_loads = [
        pltpu.make_async_copy(
            wd_hbm.at[:, columns(part)], wd_s.at[pl.ds(part * hidden, hidden)],
            load_sem.at[first + 2 * SUB + part],
        )
        for part in range(SUB)
    ]
    for load in small + inputs[0]:
        load.start()

    barrier = pltpu.get_barrier_semaphore()

    def greet(section, at):
        pl.semaphore_signal(barrier, inc=1, device_id=(section, at), device_id_type=MESH)

    greet(p, hi * PAIR + other)
    each(high - 1, lambda k: greet(p, lax.rem(hi + k + 1, high) * PAIR + lo))
    each(high, lambda k: greet(after, lax.rem(hi + k, high) * PAIR + lo))
    each(high, lambda k: greet(before, lax.rem(hi + k, high) * PAIR + lo))

    for load in inputs[1] + up_loads + down_loads + saved_load:
        load.start()

    for load in small:
        load.wait()
    tables = [route_tables(route_s[d], score_s[d], groups) for d in range(2)]
    block_rows = CAP * SUB
    for d in range(2):
        for group in range(groups):
            table_s[d, pl.ds(group * block_rows, block_rows), :] = tables[d][1][group]

    def z_copy(d, k):
        to = lax.rem(hi + k, high)
        return pltpu.make_async_remote_copy(
            slots.at[d, to // per_group], rows.at[d, hi, lo],
            z_send.at[d, k], z_recv.at[d, k], (works_for[d], to * PAIR + lo), MESH,
        )

    def y_copy(d, k, side):
        block = lax.rem(hi + high - k, high)
        return pltpu.make_async_remote_copy(
            rows.at[d, block, side], rows.at[d, block, side],
            y_send.at[d, k], y_recv.at[d, k], (p, hi * PAIR + other), MESH,
        )

    saved_copy = pltpu.make_async_remote_copy(saved_s, saved_in, s_send, s_recv, (before, e), MESH)

    def t_copy(d):
        return pltpu.make_async_remote_copy(
            table_s.at[d], table_in.at[d], t_send.at[d], t_recv.at[d], (ahead[d], e), MESH
        )

    lanes = SUB * count
    own_part = lax.broadcasted_iota(jnp.int32, (block_rows, lanes), 0) & (SUB - 1)
    same_part = own_part == lax.broadcasted_iota(jnp.int32, (block_rows, lanes), 1) // count

    def pick(d):
        chosen = []
        for group in range(groups):
            wide = jnp.concatenate([tables[d][0][group]] * SUB, axis=1)
            chosen.append(jnp.where(same_part, wide, 0.0).astype(BF))
        for load in inputs[d]:
            load.wait()
        for group in range(groups):
            slots[d, group] = jnp.dot(
                chosen[group], tokens_s[d], preferred_element_type=F32
            ).astype(BF)

    pick(0)
    rows[0, hi, lo] = slots[0, hi // per_group]
    pl.semaphore_wait(barrier, PAIR - 1 + 3 * high - 1)
    each(high - 1, lambda k: z_copy(0, k + 1).start())
    y_copy(0, 0, lo).start()
    pick(1)

    def relay(d):
        def step(k):
            z_copy(d, k + 1 - d).wait_recv()
            y_copy(d, k + 1 - d, lo).start()
        each(high - 1 + d, step)

    def gathered(d):
        each(high, lambda k: y_copy(d, k, other).wait_recv())

    step_high = min(high, 4)
    chunks = high // step_high
    blocks = step_high * PAIR
    full = blocks * block_rows
    half = step_high * block_rows

    def spread(value):
        size, wide = value.shape
        summed = jnp.sum(value.reshape(size // SUB, SUB, wide), axis=1, keepdims=True)
        return jnp.broadcast_to(summed, (size // SUB, SUB, wide)).reshape(size, wide)

    def at_chunk(chunk):
        return pl.ds(chunk * step_high, step_high)

    def forward_hidden(chunk):
        held = rows[0, at_chunk(chunk)].reshape(blocks, block_rows, width)
        acc = jnp.zeros((full, 2 * hidden), F32)
        for part, mask in enumerate(masks(width)):
            acc += jnp.dot(
                masked(held, mask), wgu_s[:, pl.ds(part * 2 * hidden, 2 * hidden)],
                preferred_element_type=F32,
            )
        pre = spread(acc)
        gate, up = pre[:, :hidden], pre[:, hidden:]
        value = (gate / (1.0 + jnp.exp(-gate)) * up).astype(BF)
        hid[at_chunk(chunk)] = value.reshape(step_high, PAIR, block_rows, hidden)

    def backward_hidden(chunk):
        held = rows[1, at_chunk(chunk)].reshape(blocks, block_rows, width)
        acc = jnp.zeros((full, hidden), F32)
        for part, mask in enumerate(masks(width)):
            acc += lax.dot_general(
                masked(held, mask), wd_s[pl.ds(part * hidden, hidden), :], NT,
                preferred_element_type=F32,
            )
        grad_hidden = spread(acc)
        size = step_high * PAIR * CAP
        kept = saved_in[pl.ds(chunk * size, size)]
        gate = jnp.broadcast_to(kept[:, 0:1, :], (size, SUB, hidden)).reshape(full, hidden)
        up = jnp.broadcast_to(kept[:, 1:2, :], (size, SUB, hidden)).reshape(full, hidden)
        sigma = 1.0 / (1.0 + jnp.exp(-gate))
        grad_gate = (grad_hidden * up * sigma * (1.0 + gate * (1.0 - sigma))).astype(BF)
        grad_up = (grad_hidden * gate * sigma).astype(BF)
        both = jnp.concatenate([grad_gate, grad_up], axis=1)
        grad[at_chunk(chunk)] = both.reshape(step_high, PAIR, block_rows, 2 * hidden)

    def side_parts(source, chunk):
        held = jnp.concatenate([source[at_chunk(chunk), other], source[at_chunk(chunk), lo]], axis=0)
        wide = held.shape[-1]
        for part, mask in enumerate(masks(wide)):
            parts_s[pl.ds(chunk * full, full), pl.ds(part * wide, wide)] = masked(held, mask)

    def forward_out(chunk, cut):
        held = parts_s[pl.ds(chunk * full, full), pl.ds(0, SUB * hidden)]
        return jnp.dot(held, wd_s[:, cut], preferred_element_type=F32)

    def backward_out(chunk, cut):
        held = parts_s[pl.ds(chunk * full, full), :]
        return lax.dot_general(held, wgu_s[cut, :], NT, preferred_element_type=F32)

    outs = (forward_out, backward_out)
    cuts = [pl.ds(low, size) for low, size in lane_chunks]

    def a_copy(d, n):
        return pltpu.make_async_remote_copy(
            away.at[d, :, :, cuts[n]], pair_in.at[d, :, :, cuts[n]],
            a_send.at[d, n], a_recv.at[d, n], (p, hi * PAIR + other), MESH,
        )

    def f_copy(d, n, k, arriving=False):
        block = lax.rem(hi + (high - k if arriving else k), high)
        slot = block if arriving else hi
        return pltpu.make_async_remote_copy(
            pair_out.at[d, block, :, cuts[n]], final_in.at[d, slot, :, cuts[n]],
            f_send.at[d, n, k], f_recv.at[d, n, k], (gives_to[d], block * PAIR + lo), MESH,
        )

    def partial(d):
        each(chunks, lambda chunk: side_parts((hid, grad)[d], chunk))
        for n, cut in enumerate(cuts):
            def make(chunk, cut=cut):
                value = outs[d](chunk, cut)
                shape = (step_high, block_rows, value.shape[1])
                away[d, at_chunk(chunk), :, cut] = value[:half].astype(BF).reshape(shape)
                mine[d, at_chunk(chunk), :, cut] = value[half:].reshape(shape)
            each(chunks, make)
            a_copy(d, n).start()

    def pass_on(d):
        for n, cut in enumerate(cuts):
            a_copy(d, n).wait_recv()

            def add(block, cut=cut):
                return (mine[d, block, :, cut] + pair_in[d, block, :, cut].astype(F32)).astype(BF)

            def send(k, n=n, cut=cut):
                block = lax.rem(hi + k + d, high)
                pair_out[d, block, :, cut] = add(block)
                f_copy(d, n, k + d).start()
            each(high - d, send)
            if d:
                final_in[d, hi, :, cut] = add(hi)

    def route_columns(d):
        t_copy(d).wait_recv()
        size = table_in.shape[1]
        row = lax.broadcasted_iota(jnp.int32, (size, size), 0)
        col = lax.broadcasted_iota(jnp.int32, (size, size), 1)
        return lax.dot_general(
            table_in[d], (row == col).astype(F32), TN,
            precision=lax.Precision.HIGHEST, preferred_element_type=F32,
        )

    def finish(d, table):
        for n in range(len(cuts)):
            each(high - d, lambda k, n=n: f_copy(d, n, k + d, True).wait_recv())
        totals = []
        for group in range(groups):
            acc = final_in[d, group * per_group].astype(F32)
            for at in range(1, per_group):
                acc += final_in[d, group * per_group + at].astype(F32)
            totals.append(acc)
        for part in range(SUB):
            acc = None
            for group in range(groups):
                for slot in range(CAP):
                    at = slot * SUB + part
                    column = group * block_rows + slot * SUB
                    term = table[:, column:column + 1] * totals[group][at:at + 1, :]
                    acc = term if acc is None else acc + term
            routed = acc.astype(BF)
            if d == 0:
                routed_s[:, columns(part)] = routed
            else:
                out_s[:, columns(part)] = (
                    routed_s[:, columns(part)].astype(F32) + routed.astype(F32)
                ).astype(BF)
                out_copy(part).start()

    def out_copy(part):
        return pltpu.make_async_copy(
            out_s.at[:, columns(part)], out_hbm.at[:, columns(part)], out_sem.at[part]
        )

    relay(0)
    for load in saved_load:
        load.wait()
    each(high, lambda k: z_copy(1, k).start())
    saved_copy.start()
    for d in range(2):
        t_copy(d).start()
    for load in up_loads:
        load.wait()
    gathered(0)
    each(chunks, forward_hidden)
    relay(1)
    for load in down_loads:
        load.wait()
    partial(0)
    gathered(1)
    saved_copy.wait_recv()
    each(chunks, backward_hidden)
    pass_on(0)
    partial(1)
    table_f, table_b = route_columns(0), route_columns(1)
    pass_on(1)
    finish(0, table_f)
    finish(1, table_b)

    for d in range(2):
        t_copy(d).wait_send()
        each(high - 1 + d, lambda k, d=d: z_copy(d, k + 1 - d).wait_send())
        each(high, lambda k, d=d: y_copy(d, k, lo).wait_send())
        for n in range(len(cuts)):
            a_copy(d, n).wait_send()
            each(high - d, lambda k, d=d, n=n: f_copy(d, n, k + d).wait_send())
    saved_copy.wait_send()
    for part in range(SUB):
        out_copy(part).wait()


def write_kernel(value_hbm, out_hbm, sem):
    tokens, model = value_hbm.shape
    high, wide = tokens // sem.shape[0], model // sem.shape[1]
    copies = []
    for at in range(sem.shape[0]):
        for side in range(sem.shape[1]):
            place = (pl.ds(at * high, high), pl.ds(side * wide, wide))
            copies.append(pltpu.make_async_copy(value_hbm.at[place], out_hbm.at[place], sem.at[at, side]))
    for copy in copies:
        copy.start()
    for copy in copies:
        copy.wait()


def solution(mesh):
    sections, ep = mesh.shape["pp"], mesh.shape["ep"]
    groups = ep // SPLIT
    high = ep // PAIR

    def body(x, dy, rf, rb, sf, sb, saved, wg, wu, wd):
        _, tokens, model = x.shape
        topk = rf.shape[2]
        hidden = wg.shape[1]
        width = model // SUB
        block_rows = CAP * SUB
        lane_chunks = [(low, min(256, width - low)) for low in range(0, width, 256)]
        cuts = len(lane_chunks)
        anywhere = pl.BlockSpec(memory_space=pl.ANY)
        out = pl.pallas_call(
            functools.partial(kernel, (sections, ep), groups, lane_chunks),
            out_shape=jax.ShapeDtypeStruct((tokens, model), BF),
            in_specs=[anywhere] * 10,
            out_specs=anywhere,
            scratch_shapes=[
                pltpu.VMEM((2, SUB * tokens, width), BF),
                pltpu.VMEM((2, topk, tokens), jnp.int32),
                pltpu.VMEM((2, topk, tokens), F32),
                pltpu.VMEM((ep * CAP, 2, hidden), F32),
                pltpu.VMEM((width, SUB * 2 * hidden), BF),
                pltpu.VMEM((SUB * hidden, width), BF),
                pltpu.VMEM((ep * CAP, 2, hidden), F32),
                pltpu.VMEM((2, groups, block_rows, width), BF),
                pltpu.VMEM((2, high, PAIR, block_rows, width), BF),
                pltpu.VMEM((high, PAIR, block_rows, hidden), BF),
                pltpu.VMEM((high, PAIR, block_rows, 2 * hidden), BF),
                pltpu.VMEM((ep * block_rows, SUB * 2 * hidden), BF),
                pltpu.VMEM((2, high, block_rows, width), BF),
                pltpu.VMEM((2, high, block_rows, width), F32),
                pltpu.VMEM((2, high, block_rows, width), BF),
                pltpu.VMEM((2, high, block_rows, width), BF),
                pltpu.VMEM((2, high, block_rows, width), BF),
                pltpu.VMEM((2, groups * block_rows, tokens), F32),
                pltpu.VMEM((2, groups * block_rows, tokens), F32),
                pltpu.VMEM((tokens, model), BF),
                pltpu.VMEM((tokens, model), BF),
                pltpu.SemaphoreType.DMA((5 + 5 * SUB,)),
                pltpu.SemaphoreType.DMA((SUB,)),
            ]
            + [pltpu.SemaphoreType.DMA((2, high))] * 4
            + [pltpu.SemaphoreType.DMA((2, cuts))] * 2
            + [pltpu.SemaphoreType.DMA((2, cuts, high))] * 2
            + [pltpu.SemaphoreType.DMA((2,))] * 2
            + [pltpu.SemaphoreType.DMA] * 2,
            compiler_params=pltpu.CompilerParams(
                collective_id=0, has_side_effects=True, vmem_limit_bytes=VMEM_BYTES
            ),
            name="experts",
        )(
            x[0], dy[0], rf[0].T, rb[0].T, sf[0].T, sb[0].T,
            saved.reshape(ep * CAP, 2, hidden), wg, wu, wd,
        )
        out = pl.pallas_call(
            write_kernel,
            out_shape=jax.ShapeDtypeStruct((tokens, model), BF),
            in_specs=[anywhere],
            out_specs=anywhere,
            scratch_shapes=[pltpu.SemaphoreType.DMA((tokens // block_rows, 2))],
            compiler_params=pltpu.CompilerParams(vmem_limit_bytes=VMEM_BYTES),
            name="write",
        )(out)
        return out[None]

    in_specs = (
        P("pp", "ep", None),
        P("pp", "ep", None),
        P("pp", "ep", None),
        P("pp", "ep", None),
        P("pp", "ep", None),
        P("pp", "ep", None),
        P("pp", None, None, None, "ep"),
        P(None, "ep"),
        P(None, "ep"),
        P("ep", None),
    )
    out_specs = P("pp", "ep", None)
    return jax.shard_map(body, mesh=mesh, in_specs=in_specs, out_specs=out_specs, check_vma=False)
```

```python
import functools

import jax
import jax.numpy as jnp
from jax import lax
from jax.experimental import pallas as pl
from jax.experimental.pallas import tpu as pltpu
from jax.sharding import PartitionSpec as P

SPLIT = 8
CAP = 2
SUB = 8
PAIR = 2
VMEM_BYTES = 60 * 1024 * 1024
MESH = pl.DeviceIdType.MESH
BF = jnp.bfloat16
F32 = jnp.float32
NT = (((1,), (1,)), ((), ()))
TN = (((0,), (0,)), ((), ()))


def each(count, step):
    if count <= 4:
        for at in range(count):
            step(at)
    else:
        lax.fori_loop(0, count, lambda at, carry: (step(at), carry)[1], 0)


def route_tables(routes, scores, groups):
    tokens = routes.shape[1]
    weight = 2.5 * scores / jnp.sum(scores, axis=0, keepdims=True)
    earlier = lax.broadcasted_iota(jnp.int32, (tokens, tokens), 0)
    later = lax.broadcasted_iota(jnp.int32, (tokens, tokens), 1)
    order = (earlier < later).astype(F32)
    rows = CAP * SUB
    slot = (lax.broadcasted_iota(jnp.int32, (rows, tokens), 0) // SUB).astype(F32)
    placed, weighted = [], []
    for group in range(groups):
        match = (routes == group).astype(F32)
        hits = jnp.broadcast_to(jnp.sum(match, axis=0, keepdims=True), (rows, tokens))
        shares = jnp.broadcast_to(jnp.sum(match * weight, axis=0, keepdims=True), (rows, tokens))
        before = jnp.dot(hits, order, preferred_element_type=F32)
        here = hits * (before == slot).astype(F32)
        placed.append(here)
        weighted.append(here * shares)
    return placed, weighted


def masks(lanes):
    part = lax.broadcasted_iota(jnp.int32, (CAP * SUB, lanes), 0) & (SUB - 1)
    return [part == at for at in range(SUB)]


def masked(held, mask):
    blocks, rows, lanes = held.shape
    return jnp.where(mask[None], held, jnp.zeros_like(held)).reshape(blocks * rows, lanes)


def kernel(
    axes, groups, lane_chunks,
    x_hbm, dy_hbm, rf_hbm, rb_hbm, sf_hbm, sb_hbm, saved_hbm, wg_hbm, wu_hbm, wd_hbm,
    out_hbm,
    tokens_s, route_s, score_s, saved_s, wgu_s, wd_s,
    saved_in, slots, rows, hid, grad, parts_s, away, mine, pair_in, pair_out, final_in, table_s, table_in, routed_s, out_s,
    load_sem, out_sem, z_send, z_recv, y_send, y_recv, a_send, a_recv, f_send, f_recv, t_send, t_recv, s_send, s_recv,
):
    sections, ep = axes
    high = ep // PAIR
    per_group = SPLIT // PAIR
    width = slots.shape[-1]
    count = x_hbm.shape[0]
    hidden = wd_s.shape[0] // SUB
    p = lax.axis_index("pp")
    e = lax.axis_index("ep")
    hi, lo = e // PAIR, lax.rem(e, PAIR)
    other = 1 - lo
    after, before = lax.rem(p + 1, sections), lax.rem(p + sections - 1, sections)
    ahead = (after, before)
    works_for = (p, before)
    gives_to = (after, p)

    def columns(part):
        return pl.ds(part * width, width)

    small = [
        pltpu.make_async_copy(rf_hbm, route_s.at[0], load_sem.at[0]),
        pltpu.make_async_copy(rb_hbm, route_s.at[1], load_sem.at[1]),
        pltpu.make_async_copy(sf_hbm, score_s.at[0], load_sem.at[2]),
        pltpu.make_async_copy(sb_hbm, score_s.at[1], load_sem.at[3]),
    ]
    inputs = [
        [
            pltpu.make_async_copy(
                hbm.at[:, columns(part)], tokens_s.at[d, pl.ds(part * count, count)],
                load_sem.at[4 + d * SUB + part],
            )
            for part in range(SUB)
        ]
        for d, hbm in enumerate((x_hbm, dy_hbm))
    ]
    first = 4 + 2 * SUB
    saved_load = [pltpu.make_async_copy(saved_hbm, saved_s, load_sem.at[first + 3 * SUB])]
    up_loads = [
        pltpu.make_async_copy(
            hbm.at[columns(part), :],
            wgu_s.at[:, pl.ds((2 * part + side) * hidden, hidden)],
            load_sem.at[first + side * SUB + part],
        )
        for part in range(SUB)
        for side, hbm in enumerate((wg_hbm, wu_hbm))
    ]
    down_loads = [
        pltpu.make_async_copy(
            wd_hbm.at[:, columns(part)], wd_s.at[pl.ds(part * hidden, hidden)],
            load_sem.at[first + 2 * SUB + part],
        )
        for part in range(SUB)
    ]
    for load in small + inputs[0]:
        load.start()

    barrier = pltpu.get_barrier_semaphore()

    def greet(section, at):
        pl.semaphore_signal(barrier, inc=1, device_id=(section, at), device_id_type=MESH)

    greet(p, hi * PAIR + other)
    each(high - 1, lambda k: greet(p, lax.rem(hi + k + 1, high) * PAIR + lo))
    each(high, lambda k: greet(after, lax.rem(hi + k, high) * PAIR + lo))
    each(high, lambda k: greet(before, lax.rem(hi + k, high) * PAIR + lo))

    for load in inputs[1]:
        load.start()

    for load in small:
        load.wait()
    tables = [route_tables(route_s[d], score_s[d], groups) for d in range(2)]
    block_rows = CAP * SUB
    for d in range(2):
        for group in range(groups):
            table_s[d, pl.ds(group * block_rows, block_rows), :] = tables[d][1][group]

    def z_copy(d, k):
        to = lax.rem(hi + k, high)
        return pltpu.make_async_remote_copy(
            slots.at[d, to // per_group], rows.at[d, hi, lo],
            z_send.at[d, k], z_recv.at[d, k], (works_for[d], to * PAIR + lo), MESH,
        )

    def y_copy(d, k, side):
        block = lax.rem(hi + high - k, high)
        return pltpu.make_async_remote_copy(
            rows.at[d, block, side], rows.at[d, block, side],
            y_send.at[d, k], y_recv.at[d, k], (p, hi * PAIR + other), MESH,
        )

    saved_copy = pltpu.make_async_remote_copy(saved_s, saved_in, s_send, s_recv, (before, e), MESH)

    def t_copy(d):
        return pltpu.make_async_remote_copy(
            table_s.at[d], table_in.at[d], t_send.at[d], t_recv.at[d], (ahead[d], e), MESH
        )

    lanes = SUB * count
    own_part = lax.broadcasted_iota(jnp.int32, (block_rows, lanes), 0) & (SUB - 1)
    same_part = own_part == lax.broadcasted_iota(jnp.int32, (block_rows, lanes), 1) // count

    def pick(d):
        chosen = []
        for group in range(groups):
            wide = jnp.concatenate([tables[d][0][group]] * SUB, axis=1)
            chosen.append(jnp.where(same_part, wide, 0.0).astype(BF))
        for load in inputs[d]:
            load.wait()
        for group in range(groups):
            slots[d, group] = jnp.dot(
                chosen[group], tokens_s[d], preferred_element_type=F32
            ).astype(BF)

    pick(0)
    rows[0, hi, lo] = slots[0, hi // per_group]
    pl.semaphore_wait(barrier, PAIR - 1 + 3 * high - 1)
    each(high - 1, lambda k: z_copy(0, k + 1).start())
    y_copy(0, 0, lo).start()
    for load in saved_load + up_loads + down_loads:
        load.start()
    pick(1)
    each(high, lambda k: z_copy(1, k).start())
    for load in saved_load:
        load.wait()
    saved_copy.start()

    def relay(d):
        def step(k):
            z_copy(d, k + 1 - d).wait_recv()
            y_copy(d, k + 1 - d, lo).start()
        each(high - 1 + d, step)

    def gathered(d):
        each(high, lambda k: y_copy(d, k, other).wait_recv())

    step_high = min(high, 4)
    chunks = high // step_high
    blocks = step_high * PAIR
    full = blocks * block_rows
    half = step_high * block_rows

    def spread(value):
        size, wide = value.shape
        summed = jnp.sum(value.reshape(size // SUB, SUB, wide), axis=1, keepdims=True)
        return jnp.broadcast_to(summed, (size // SUB, SUB, wide)).reshape(size, wide)

    def at_chunk(chunk):
        return pl.ds(chunk * step_high, step_high)

    def forward_hidden(chunk):
        held = rows[0, at_chunk(chunk)].reshape(blocks, block_rows, width)
        acc = jnp.zeros((full, 2 * hidden), F32)
        for part, mask in enumerate(masks(width)):
            acc += jnp.dot(
                masked(held, mask), wgu_s[:, pl.ds(part * 2 * hidden, 2 * hidden)],
                preferred_element_type=F32,
            )
        pre = spread(acc)
        gate, up = pre[:, :hidden], pre[:, hidden:]
        value = (gate / (1.0 + jnp.exp(-gate)) * up).astype(BF)
        hid[at_chunk(chunk)] = value.reshape(step_high, PAIR, block_rows, hidden)

    def backward_hidden(chunk):
        held = rows[1, at_chunk(chunk)].reshape(blocks, block_rows, width)
        acc = jnp.zeros((full, hidden), F32)
        for part, mask in enumerate(masks(width)):
            acc += lax.dot_general(
                masked(held, mask), wd_s[pl.ds(part * hidden, hidden), :], NT,
                preferred_element_type=F32,
            )
        grad_hidden = spread(acc)
        size = step_high * PAIR * CAP
        kept = saved_in[pl.ds(chunk * size, size)]
        gate = jnp.broadcast_to(kept[:, 0:1, :], (size, SUB, hidden)).reshape(full, hidden)
        up = jnp.broadcast_to(kept[:, 1:2, :], (size, SUB, hidden)).reshape(full, hidden)
        sigma = 1.0 / (1.0 + jnp.exp(-gate))
        grad_gate = (grad_hidden * up * sigma * (1.0 + gate * (1.0 - sigma))).astype(BF)
        grad_up = (grad_hidden * gate * sigma).astype(BF)
        both = jnp.concatenate([grad_gate, grad_up], axis=1)
        grad[at_chunk(chunk)] = both.reshape(step_high, PAIR, block_rows, 2 * hidden)

    def side_parts(source, chunk):
        held = jnp.concatenate([source[at_chunk(chunk), other], source[at_chunk(chunk), lo]], axis=0)
        wide = held.shape[-1]
        for part, mask in enumerate(masks(wide)):
            parts_s[pl.ds(chunk * full, full), pl.ds(part * wide, wide)] = masked(held, mask)

    def forward_out(chunk, cut):
        held = parts_s[pl.ds(chunk * full, full), pl.ds(0, SUB * hidden)]
        return jnp.dot(held, wd_s[:, cut], preferred_element_type=F32)

    def backward_out(chunk, cut):
        held = parts_s[pl.ds(chunk * full, full), :]
        return lax.dot_general(held, wgu_s[cut, :], NT, preferred_element_type=F32)

    outs = (forward_out, backward_out)
    cuts = [pl.ds(low, size) for low, size in lane_chunks]

    def a_copy(d, n):
        return pltpu.make_async_remote_copy(
            away.at[d, :, :, cuts[n]], pair_in.at[d, :, :, cuts[n]],
            a_send.at[d, n], a_recv.at[d, n], (p, hi * PAIR + other), MESH,
        )

    def f_copy(d, n, k, arriving=False):
        block = lax.rem(hi + (high - k if arriving else k), high)
        slot = block if arriving else hi
        return pltpu.make_async_remote_copy(
            pair_out.at[d, block, :, cuts[n]], final_in.at[d, slot, :, cuts[n]],
            f_send.at[d, n, k], f_recv.at[d, n, k], (gives_to[d], block * PAIR + lo), MESH,
        )

    def partial(d):
        each(chunks, lambda chunk: side_parts((hid, grad)[d], chunk))
        for n, cut in enumerate(cuts):
            def make(chunk, cut=cut):
                value = outs[d](chunk, cut)
                shape = (step_high, block_rows, value.shape[1])
                away[d, at_chunk(chunk), :, cut] = value[:half].astype(BF).reshape(shape)
                mine[d, at_chunk(chunk), :, cut] = value[half:].reshape(shape)
            each(chunks, make)
            a_copy(d, n).start()

    def pass_on(d):
        for n, cut in enumerate(cuts):
            a_copy(d, n).wait_recv()

            def add(block, cut=cut):
                return (mine[d, block, :, cut] + pair_in[d, block, :, cut].astype(F32)).astype(BF)

            def send(k, n=n, cut=cut):
                block = lax.rem(hi + k + d, high)
                pair_out[d, block, :, cut] = add(block)
                f_copy(d, n, k + d).start()
            each(high - d, send)
            if d:
                final_in[d, hi, :, cut] = add(hi)

    def route_columns(d):
        t_copy(d).wait_recv()
        size = table_in.shape[1]
        row = lax.broadcasted_iota(jnp.int32, (size, size), 0)
        col = lax.broadcasted_iota(jnp.int32, (size, size), 1)
        return lax.dot_general(
            table_in[d], (row == col).astype(F32), TN,
            precision=lax.Precision.HIGHEST, preferred_element_type=F32,
        )

    def finish(d, table):
        for n in range(len(cuts)):
            each(high - d, lambda k, n=n: f_copy(d, n, k + d, True).wait_recv())
        totals = []
        for group in range(groups):
            acc = final_in[d, group * per_group].astype(F32)
            for at in range(1, per_group):
                acc += final_in[d, group * per_group + at].astype(F32)
            totals.append(acc)
        for part in range(SUB):
            acc = None
            for group in range(groups):
                for slot in range(CAP):
                    at = slot * SUB + part
                    column = group * block_rows + slot * SUB
                    term = table[:, column:column + 1] * totals[group][at:at + 1, :]
                    acc = term if acc is None else acc + term
            routed = acc.astype(BF)
            if d == 0:
                routed_s[:, columns(part)] = routed
            else:
                out_s[:, columns(part)] = (
                    routed_s[:, columns(part)].astype(F32) + routed.astype(F32)
                ).astype(BF)
                out_copy(part).start()

    def out_copy(part):
        return pltpu.make_async_copy(
            out_s.at[:, columns(part)], out_hbm.at[:, columns(part)], out_sem.at[part]
        )

    relay(0)
    for d in range(2):
        t_copy(d).start()
    for load in up_loads:
        load.wait()
    gathered(0)
    each(chunks, forward_hidden)
    relay(1)
    for load in down_loads:
        load.wait()
    partial(0)
    gathered(1)
    saved_copy.wait_recv()
    each(chunks, backward_hidden)
    pass_on(0)
    partial(1)
    table_f, table_b = route_columns(0), route_columns(1)
    pass_on(1)
    finish(0, table_f)
    finish(1, table_b)

    for d in range(2):
        t_copy(d).wait_send()
        each(high - 1 + d, lambda k, d=d: z_copy(d, k + 1 - d).wait_send())
        each(high, lambda k, d=d: y_copy(d, k, lo).wait_send())
        for n in range(len(cuts)):
            a_copy(d, n).wait_send()
            each(high - d, lambda k, d=d, n=n: f_copy(d, n, k + d).wait_send())
    saved_copy.wait_send()
    for part in range(SUB):
        out_copy(part).wait()


def write_kernel(value_hbm, out_hbm, held, load_sem, store_sem):
    wide = value_hbm.shape[1] // SUB
    loads, stores = [], []
    for at in range(SUB):
        place = (slice(None), pl.ds(at * wide, wide))
        loads.append(pltpu.make_async_copy(value_hbm.at[place], held.at[at], load_sem.at[at]))
        stores.append(pltpu.make_async_copy(held.at[at], out_hbm.at[place], store_sem.at[at]))
        loads[at].start()
    for at in range(SUB):
        loads[at].wait()
        stores[at].start()
    for store in stores:
        store.wait()


def solution(mesh):
    sections, ep = mesh.shape["pp"], mesh.shape["ep"]
    groups = ep // SPLIT
    high = ep // PAIR

    def body(x, dy, rf, rb, sf, sb, saved, wg, wu, wd):
        _, tokens, model = x.shape
        topk = rf.shape[2]
        hidden = wg.shape[1]
        width = model // SUB
        block_rows = CAP * SUB
        lane_chunks = [(low, min(256, width - low)) for low in range(0, width, 256)]
        cuts = len(lane_chunks)
        anywhere = pl.BlockSpec(memory_space=pl.ANY)
        out = pl.pallas_call(
            functools.partial(kernel, (sections, ep), groups, lane_chunks),
            out_shape=jax.ShapeDtypeStruct((tokens, model), BF),
            in_specs=[anywhere] * 10,
            out_specs=anywhere,
            scratch_shapes=[
                pltpu.VMEM((2, SUB * tokens, width), BF),
                pltpu.VMEM((2, topk, tokens), jnp.int32),
                pltpu.VMEM((2, topk, tokens), F32),
                pltpu.VMEM((ep * CAP, 2, hidden), F32),
                pltpu.VMEM((width, SUB * 2 * hidden), BF),
                pltpu.VMEM((SUB * hidden, width), BF),
                pltpu.VMEM((ep * CAP, 2, hidden), F32),
                pltpu.VMEM((2, groups, block_rows, width), BF),
                pltpu.VMEM((2, high, PAIR, block_rows, width), BF),
                pltpu.VMEM((high, PAIR, block_rows, hidden), BF),
                pltpu.VMEM((high, PAIR, block_rows, 2 * hidden), BF),
                pltpu.VMEM((ep * block_rows, SUB * 2 * hidden), BF),
                pltpu.VMEM((2, high, block_rows, width), BF),
                pltpu.VMEM((2, high, block_rows, width), F32),
                pltpu.VMEM((2, high, block_rows, width), BF),
                pltpu.VMEM((2, high, block_rows, width), BF),
                pltpu.VMEM((2, high, block_rows, width), BF),
                pltpu.VMEM((2, groups * block_rows, tokens), F32),
                pltpu.VMEM((2, groups * block_rows, tokens), F32),
                pltpu.VMEM((tokens, model), BF),
                pltpu.VMEM((tokens, model), BF),
                pltpu.SemaphoreType.DMA((5 + 5 * SUB,)),
                pltpu.SemaphoreType.DMA((SUB,)),
            ]
            + [pltpu.SemaphoreType.DMA((2, high))] * 4
            + [pltpu.SemaphoreType.DMA((2, cuts))] * 2
            + [pltpu.SemaphoreType.DMA((2, cuts, high))] * 2
            + [pltpu.SemaphoreType.DMA((2,))] * 2
            + [pltpu.SemaphoreType.DMA] * 2,
            compiler_params=pltpu.CompilerParams(
                collective_id=0, has_side_effects=True, vmem_limit_bytes=VMEM_BYTES
            ),
            name="experts",
        )(
            x[0], dy[0], rf[0].T, rb[0].T, sf[0].T, sb[0].T,
            saved.reshape(ep * CAP, 2, hidden), wg, wu, wd,
        )
        out = pl.pallas_call(
            write_kernel,
            out_shape=jax.ShapeDtypeStruct((tokens, model), BF),
            in_specs=[anywhere],
            out_specs=anywhere,
            scratch_shapes=[
                pltpu.VMEM((SUB, tokens, width), BF),
                pltpu.SemaphoreType.DMA((SUB,)),
                pltpu.SemaphoreType.DMA((SUB,)),
            ],
            compiler_params=pltpu.CompilerParams(vmem_limit_bytes=VMEM_BYTES),
            name="write",
        )(out)
        return out[None]

    in_specs = (
        P("pp", "ep", None),
        P("pp", "ep", None),
        P("pp", "ep", None),
        P("pp", "ep", None),
        P("pp", "ep", None),
        P("pp", "ep", None),
        P("pp", None, None, None, "ep"),
        P(None, "ep"),
        P(None, "ep"),
        P("ep", None),
    )
    out_specs = P("pp", "ep", None)
    return jax.shard_map(body, mesh=mesh, in_specs=in_specs, out_specs=out_specs, check_vma=False)
```

```python
import functools

import jax
import jax.numpy as jnp
from jax import lax
from jax.experimental import pallas as pl
from jax.experimental.pallas import tpu as pltpu
from jax.sharding import PartitionSpec as P

SPLIT = 8
CAP = 2
SUB = 8
PAIR = 2
VMEM_BYTES = 60 * 1024 * 1024
MESH = pl.DeviceIdType.MESH
BF = jnp.bfloat16
F32 = jnp.float32
NT = (((1,), (1,)), ((), ()))
TN = (((0,), (0,)), ((), ()))


def each(count, step):
    if count <= 4:
        for at in range(count):
            step(at)
    else:
        lax.fori_loop(0, count, lambda at, carry: (step(at), carry)[1], 0)


def route_tables(routes, scores, groups):
    tokens = routes.shape[1]
    weight = 2.5 * scores / jnp.sum(scores, axis=0, keepdims=True)
    earlier = lax.broadcasted_iota(jnp.int32, (tokens, tokens), 0)
    later = lax.broadcasted_iota(jnp.int32, (tokens, tokens), 1)
    order = (earlier < later).astype(F32)
    rows = CAP * SUB
    slot = (lax.broadcasted_iota(jnp.int32, (rows, tokens), 0) // SUB).astype(F32)
    placed, weighted = [], []
    for group in range(groups):
        match = (routes == group).astype(F32)
        hits = jnp.broadcast_to(jnp.sum(match, axis=0, keepdims=True), (rows, tokens))
        shares = jnp.broadcast_to(jnp.sum(match * weight, axis=0, keepdims=True), (rows, tokens))
        before = jnp.dot(hits, order, preferred_element_type=F32)
        here = hits * (before == slot).astype(F32)
        placed.append(here)
        weighted.append(here * shares)
    return placed, weighted


def masks(lanes):
    part = lax.broadcasted_iota(jnp.int32, (CAP * SUB, lanes), 0) & (SUB - 1)
    return [part == at for at in range(SUB)]


def masked(held, mask):
    blocks, rows, lanes = held.shape
    return jnp.where(mask[None], held, jnp.zeros_like(held)).reshape(blocks * rows, lanes)


def kernel(
    axes, groups, lane_chunks,
    x_hbm, dy_hbm, rf_hbm, rb_hbm, sf_hbm, sb_hbm, saved_hbm, wg_hbm, wu_hbm, wd_hbm,
    out_hbm,
    tokens_s, route_s, score_s, saved_s, wgu_s, wd_s,
    saved_in, slots, shifted, total_s, total_in, rows, hid, grad, parts_s, away, mine, pair_in, pair_out, final_in, table_s, table_in, routed_s, out_s,
    load_sem, out_sem, z_send, z_recv, y_send, y_recv, a_send, a_recv, f_send, f_recv, t_send, t_recv, s_send, s_recv, x_send, x_recv,
):
    sections, ep = axes
    high = ep // PAIR
    per_group = SPLIT // PAIR
    width = slots.shape[-1]
    count = x_hbm.shape[0]
    hidden = wd_s.shape[0] // SUB
    p = lax.axis_index("pp")
    e = lax.axis_index("ep")
    hi, lo = e // PAIR, lax.rem(e, PAIR)
    other = 1 - lo
    after, before = lax.rem(p + 1, sections), lax.rem(p + sections - 1, sections)
    ahead = (after, before)

    def columns(part):
        return pl.ds(part * width, width)

    small = [
        pltpu.make_async_copy(rf_hbm, route_s.at[0], load_sem.at[0]),
        pltpu.make_async_copy(rb_hbm, route_s.at[1], load_sem.at[1]),
        pltpu.make_async_copy(sf_hbm, score_s.at[0], load_sem.at[2]),
        pltpu.make_async_copy(sb_hbm, score_s.at[1], load_sem.at[3]),
    ]
    inputs = [
        [
            pltpu.make_async_copy(
                hbm.at[:, columns(part)], tokens_s.at[d, pl.ds(part * count, count)],
                load_sem.at[4 + d * SUB + part],
            )
            for part in range(SUB)
        ]
        for d, hbm in enumerate((x_hbm, dy_hbm))
    ]
    first = 4 + 2 * SUB
    saved_load = [pltpu.make_async_copy(saved_hbm, saved_s, load_sem.at[first + 3 * SUB])]
    up_loads = [
        pltpu.make_async_copy(
            hbm.at[columns(part), :],
            wgu_s.at[:, pl.ds((2 * part + side) * hidden, hidden)],
            load_sem.at[first + side * SUB + part],
        )
        for part in range(SUB)
        for side, hbm in enumerate((wg_hbm, wu_hbm))
    ]
    down_loads = [
        pltpu.make_async_copy(
            wd_hbm.at[:, columns(part)], wd_s.at[pl.ds(part * hidden, hidden)],
            load_sem.at[first + 2 * SUB + part],
        )
        for part in range(SUB)
    ]
    for load in small + inputs[0]:
        load.start()

    barrier = pltpu.get_barrier_semaphore()

    def greet(section, at):
        pl.semaphore_signal(barrier, inc=1, device_id=(section, at), device_id_type=MESH)

    greet(p, hi * PAIR + other)
    each(high - 1, lambda k: greet(p, lax.rem(hi + k + 1, high) * PAIR + lo))
    greet(after, e)
    greet(before, e)

    for load in inputs[1]:
        load.start()

    for load in small:
        load.wait()
    tables = [route_tables(route_s[d], score_s[d], groups) for d in range(2)]
    block_rows = CAP * SUB
    for d in range(2):
        for group in range(groups):
            table_s[d, pl.ds(group * block_rows, block_rows), :] = tables[d][1][group]

    def z_copy(d, k):
        to = lax.rem(hi + k, high)
        source = shifted if d else slots.at[0]
        return pltpu.make_async_remote_copy(
            source.at[to // per_group], rows.at[d, hi, lo],
            z_send.at[d, k], z_recv.at[d, k], (p, to * PAIR + lo), MESH,
        )

    def y_copy(d, k, side):
        block = lax.rem(hi + high - k, high)
        return pltpu.make_async_remote_copy(
            rows.at[d, block, side], rows.at[d, block, side],
            y_send.at[d, k], y_recv.at[d, k], (p, hi * PAIR + other), MESH,
        )

    shift_copy = pltpu.make_async_remote_copy(
        slots.at[1], shifted, x_send.at[1], x_recv.at[1], (before, e), MESH
    )
    total_copy = pltpu.make_async_remote_copy(
        total_s, total_in, x_send.at[0], x_recv.at[0], (after, e), MESH
    )
    saved_copy = pltpu.make_async_remote_copy(saved_s, saved_in, s_send, s_recv, (before, e), MESH)

    def t_copy(d):
        return pltpu.make_async_remote_copy(
            table_s.at[d], table_in.at[d], t_send.at[d], t_recv.at[d], (ahead[d], e), MESH
        )

    lanes = SUB * count
    own_part = lax.broadcasted_iota(jnp.int32, (block_rows, lanes), 0) & (SUB - 1)
    same_part = own_part == lax.broadcasted_iota(jnp.int32, (block_rows, lanes), 1) // count

    def pick(d):
        chosen = []
        for group in range(groups):
            wide = jnp.concatenate([tables[d][0][group]] * SUB, axis=1)
            chosen.append(jnp.where(same_part, wide, 0.0).astype(BF))
        for load in inputs[d]:
            load.wait()
        for group in range(groups):
            slots[d, group] = jnp.dot(
                chosen[group], tokens_s[d], preferred_element_type=F32
            ).astype(BF)

    pick(0)
    rows[0, hi, lo] = slots[0, hi // per_group]
    pl.semaphore_wait(barrier, PAIR - 1 + high - 1 + 2)
    each(high - 1, lambda k: z_copy(0, k + 1).start())
    y_copy(0, 0, lo).start()
    for load in saved_load + up_loads + down_loads:
        load.start()
    pick(1)
    shift_copy.start()
    for load in saved_load:
        load.wait()
    saved_copy.start()
    shift_copy.wait_recv()
    rows[1, hi, lo] = shifted[hi // per_group]
    each(high - 1, lambda k: z_copy(1, k + 1).start())
    y_copy(1, 0, lo).start()

    def relay(d):
        def step(k):
            z_copy(d, k + 1).wait_recv()
            y_copy(d, k + 1, lo).start()
        each(high - 1, step)

    def gathered(d):
        each(high, lambda k: y_copy(d, k, other).wait_recv())

    step_high = min(high, 4)
    chunks = high // step_high
    blocks = step_high * PAIR
    full = blocks * block_rows
    half = step_high * block_rows

    def spread(value):
        size, wide = value.shape
        summed = jnp.sum(value.reshape(size // SUB, SUB, wide), axis=1, keepdims=True)
        return jnp.broadcast_to(summed, (size // SUB, SUB, wide)).reshape(size, wide)

    def at_chunk(chunk):
        return pl.ds(chunk * step_high, step_high)

    def forward_hidden(chunk):
        held = rows[0, at_chunk(chunk)].reshape(blocks, block_rows, width)
        acc = jnp.zeros((full, 2 * hidden), F32)
        for part, mask in enumerate(masks(width)):
            acc += jnp.dot(
                masked(held, mask), wgu_s[:, pl.ds(part * 2 * hidden, 2 * hidden)],
                preferred_element_type=F32,
            )
        pre = spread(acc)
        gate, up = pre[:, :hidden], pre[:, hidden:]
        value = (gate / (1.0 + jnp.exp(-gate)) * up).astype(BF)
        hid[at_chunk(chunk)] = value.reshape(step_high, PAIR, block_rows, hidden)

    def backward_hidden(chunk):
        held = rows[1, at_chunk(chunk)].reshape(blocks, block_rows, width)
        acc = jnp.zeros((full, hidden), F32)
        for part, mask in enumerate(masks(width)):
            acc += lax.dot_general(
                masked(held, mask), wd_s[pl.ds(part * hidden, hidden), :], NT,
                preferred_element_type=F32,
            )
        grad_hidden = spread(acc)
        size = step_high * PAIR * CAP
        kept = saved_in[pl.ds(chunk * size, size)]
        gate = jnp.broadcast_to(kept[:, 0:1, :], (size, SUB, hidden)).reshape(full, hidden)
        up = jnp.broadcast_to(kept[:, 1:2, :], (size, SUB, hidden)).reshape(full, hidden)
        sigma = 1.0 / (1.0 + jnp.exp(-gate))
        grad_gate = (grad_hidden * up * sigma * (1.0 + gate * (1.0 - sigma))).astype(BF)
        grad_up = (grad_hidden * gate * sigma).astype(BF)
        both = jnp.concatenate([grad_gate, grad_up], axis=1)
        grad[at_chunk(chunk)] = both.reshape(step_high, PAIR, block_rows, 2 * hidden)

    def side_parts(source, chunk):
        held = jnp.concatenate([source[at_chunk(chunk), other], source[at_chunk(chunk), lo]], axis=0)
        wide = held.shape[-1]
        for part, mask in enumerate(masks(wide)):
            parts_s[pl.ds(chunk * full, full), pl.ds(part * wide, wide)] = masked(held, mask)

    def forward_out(chunk, cut):
        held = parts_s[pl.ds(chunk * full, full), pl.ds(0, SUB * hidden)]
        return jnp.dot(held, wd_s[:, cut], preferred_element_type=F32)

    def backward_out(chunk, cut):
        held = parts_s[pl.ds(chunk * full, full), :]
        return lax.dot_general(held, wgu_s[cut, :], NT, preferred_element_type=F32)

    outs = (forward_out, backward_out)
    cuts = [pl.ds(low, size) for low, size in lane_chunks]

    def a_copy(d, n):
        return pltpu.make_async_remote_copy(
            away.at[d, :, :, cuts[n]], pair_in.at[d, :, :, cuts[n]],
            a_send.at[d, n], a_recv.at[d, n], (p, hi * PAIR + other), MESH,
        )

    def f_copy(d, n, k, arriving=False):
        block = lax.rem(hi + (high - k if arriving else k), high)
        slot = block if arriving else hi
        return pltpu.make_async_remote_copy(
            pair_out.at[d, block, :, cuts[n]], final_in.at[d, slot, :, cuts[n]],
            f_send.at[d, n, k], f_recv.at[d, n, k], (p, block * PAIR + lo), MESH,
        )

    def partial(d):
        each(chunks, lambda chunk: side_parts((hid, grad)[d], chunk))
        for n, cut in enumerate(cuts):
            def make(chunk, cut=cut):
                value = outs[d](chunk, cut)
                shape = (step_high, block_rows, value.shape[1])
                away[d, at_chunk(chunk), :, cut] = value[:half].astype(BF).reshape(shape)
                mine[d, at_chunk(chunk), :, cut] = value[half:].reshape(shape)
            each(chunks, make)
            a_copy(d, n).start()

    def pass_on(d):
        for n, cut in enumerate(cuts):
            a_copy(d, n).wait_recv()

            def add(block, cut=cut):
                return (mine[d, block, :, cut] + pair_in[d, block, :, cut].astype(F32)).astype(BF)

            def send(k, n=n, cut=cut):
                block = lax.rem(hi + k + 1, high)
                pair_out[d, block, :, cut] = add(block)
                f_copy(d, n, k + 1).start()
            each(high - 1, send)
            final_in[d, hi, :, cut] = add(hi)

    def route_columns(d):
        t_copy(d).wait_recv()
        size = table_in.shape[1]
        row = lax.broadcasted_iota(jnp.int32, (size, size), 0)
        col = lax.broadcasted_iota(jnp.int32, (size, size), 1)
        return lax.dot_general(
            table_in[d], (row == col).astype(F32), TN,
            precision=lax.Precision.HIGHEST, preferred_element_type=F32,
        )

    def total(d):
        for n in range(len(cuts)):
            each(high - 1, lambda k, n=n: f_copy(d, n, k + 1, True).wait_recv())
        sums = []
        for group in range(groups):
            acc = final_in[d, group * per_group].astype(F32)
            for at in range(1, per_group):
                acc += final_in[d, group * per_group + at].astype(F32)
            sums.append(acc)
        return sums

    def finish(d, table, totals):
        for part in range(SUB):
            acc = None
            for group in range(groups):
                for slot in range(CAP):
                    at = slot * SUB + part
                    column = group * block_rows + slot * SUB
                    term = table[:, column:column + 1] * totals[group][at:at + 1, :]
                    acc = term if acc is None else acc + term
            routed = acc.astype(BF)
            if d == 0:
                routed_s[:, columns(part)] = routed
            else:
                out_s[:, columns(part)] = (
                    routed_s[:, columns(part)].astype(F32) + routed.astype(F32)
                ).astype(BF)
                out_copy(part).start()

    def out_copy(part):
        return pltpu.make_async_copy(
            out_s.at[:, columns(part)], out_hbm.at[:, columns(part)], out_sem.at[part]
        )

    relay(0)
    for d in range(2):
        t_copy(d).start()
    for load in up_loads:
        load.wait()
    gathered(0)
    each(chunks, forward_hidden)
    relay(1)
    for load in down_loads:
        load.wait()
    partial(0)
    gathered(1)
    saved_copy.wait_recv()
    each(chunks, backward_hidden)
    pass_on(0)
    partial(1)
    table_f, table_b = route_columns(0), route_columns(1)
    for group, value in enumerate(total(0)):
        total_s[pl.ds(group * block_rows, block_rows), :] = value
    total_copy.start()
    pass_on(1)
    total_copy.wait_recv()
    finish(0, table_f, [total_in[pl.ds(group * block_rows, block_rows), :] for group in range(groups)])
    finish(1, table_b, total(1))

    for d in range(2):
        t_copy(d).wait_send()
        each(high - 1, lambda k, d=d: z_copy(d, k + 1).wait_send())
        each(high, lambda k, d=d: y_copy(d, k, lo).wait_send())
        for n in range(len(cuts)):
            a_copy(d, n).wait_send()
            each(high - 1, lambda k, d=d, n=n: f_copy(d, n, k + 1).wait_send())
    for copy in (saved_copy, shift_copy, total_copy):
        copy.wait_send()
    for part in range(SUB):
        out_copy(part).wait()


def write_kernel(value_hbm, out_hbm, held, load_sem, store_sem):
    wide = value_hbm.shape[1] // SUB
    loads, stores = [], []
    for at in range(SUB):
        place = (slice(None), pl.ds(at * wide, wide))
        loads.append(pltpu.make_async_copy(value_hbm.at[place], held.at[at], load_sem.at[at]))
        stores.append(pltpu.make_async_copy(held.at[at], out_hbm.at[place], store_sem.at[at]))
        loads[at].start()
    for at in range(SUB):
        loads[at].wait()
        stores[at].start()
    for store in stores:
        store.wait()


def solution(mesh):
    sections, ep = mesh.shape["pp"], mesh.shape["ep"]
    groups = ep // SPLIT
    high = ep // PAIR

    def body(x, dy, rf, rb, sf, sb, saved, wg, wu, wd):
        _, tokens, model = x.shape
        topk = rf.shape[2]
        hidden = wg.shape[1]
        width = model // SUB
        block_rows = CAP * SUB
        lane_chunks = [(low, min(512, width - low)) for low in range(0, width, 512)]
        cuts = len(lane_chunks)
        anywhere = pl.BlockSpec(memory_space=pl.ANY)
        out = pl.pallas_call(
            functools.partial(kernel, (sections, ep), groups, lane_chunks),
            out_shape=jax.ShapeDtypeStruct((tokens, model), BF),
            in_specs=[anywhere] * 10,
            out_specs=anywhere,
            scratch_shapes=[
                pltpu.VMEM((2, SUB * tokens, width), BF),
                pltpu.VMEM((2, topk, tokens), jnp.int32),
                pltpu.VMEM((2, topk, tokens), F32),
                pltpu.VMEM((ep * CAP, 2, hidden), F32),
                pltpu.VMEM((width, SUB * 2 * hidden), BF),
                pltpu.VMEM((SUB * hidden, width), BF),
                pltpu.VMEM((ep * CAP, 2, hidden), F32),
                pltpu.VMEM((2, groups, block_rows, width), BF),
                pltpu.VMEM((groups, block_rows, width), BF),
                pltpu.VMEM((groups * block_rows, width), F32),
                pltpu.VMEM((groups * block_rows, width), F32),
                pltpu.VMEM((2, high, PAIR, block_rows, width), BF),
                pltpu.VMEM((high, PAIR, block_rows, hidden), BF),
                pltpu.VMEM((high, PAIR, block_rows, 2 * hidden), BF),
                pltpu.VMEM((ep * block_rows, SUB * 2 * hidden), BF),
                pltpu.VMEM((2, high, block_rows, width), BF),
                pltpu.VMEM((2, high, block_rows, width), F32),
                pltpu.VMEM((2, high, block_rows, width), BF),
                pltpu.VMEM((2, high, block_rows, width), BF),
                pltpu.VMEM((2, high, block_rows, width), BF),
                pltpu.VMEM((2, groups * block_rows, tokens), F32),
                pltpu.VMEM((2, groups * block_rows, tokens), F32),
                pltpu.VMEM((tokens, model), BF),
                pltpu.VMEM((tokens, model), BF),
                pltpu.SemaphoreType.DMA((5 + 5 * SUB,)),
                pltpu.SemaphoreType.DMA((SUB,)),
            ]
            + [pltpu.SemaphoreType.DMA((2, high))] * 4
            + [pltpu.SemaphoreType.DMA((2, cuts))] * 2
            + [pltpu.SemaphoreType.DMA((2, cuts, high))] * 2
            + [pltpu.SemaphoreType.DMA((2,))] * 2
            + [pltpu.SemaphoreType.DMA] * 2
            + [pltpu.SemaphoreType.DMA((2,))] * 2,
            compiler_params=pltpu.CompilerParams(
                collective_id=0, has_side_effects=True, vmem_limit_bytes=VMEM_BYTES
            ),
            name="experts",
        )(
            x[0], dy[0], rf[0].T, rb[0].T, sf[0].T, sb[0].T,
            saved.reshape(ep * CAP, 2, hidden), wg, wu, wd,
        )
        out = pl.pallas_call(
            write_kernel,
            out_shape=jax.ShapeDtypeStruct((tokens, model), BF),
            in_specs=[anywhere],
            out_specs=anywhere,
            scratch_shapes=[
                pltpu.VMEM((SUB, tokens, width), BF),
                pltpu.SemaphoreType.DMA((SUB,)),
                pltpu.SemaphoreType.DMA((SUB,)),
            ],
            compiler_params=pltpu.CompilerParams(vmem_limit_bytes=VMEM_BYTES),
            name="write",
        )(out)
        return out[None]

    in_specs = (
        P("pp", "ep", None),
        P("pp", "ep", None),
        P("pp", "ep", None),
        P("pp", "ep", None),
        P("pp", "ep", None),
        P("pp", "ep", None),
        P("pp", None, None, None, "ep"),
        P(None, "ep"),
        P(None, "ep"),
        P("ep", None),
    )
    out_specs = P("pp", "ep", None)
    return jax.shard_map(body, mesh=mesh, in_specs=in_specs, out_specs=out_specs, check_vma=False)
```

```python
import functools

import jax
import jax.numpy as jnp
from jax import lax
from jax.experimental import pallas as pl
from jax.experimental.pallas import tpu as pltpu
from jax.sharding import PartitionSpec as P

SPLIT = 8
CAP = 2
SUB = 8
PAIR = 2
VMEM_BYTES = 60 * 1024 * 1024
MESH = pl.DeviceIdType.MESH
BF = jnp.bfloat16
F32 = jnp.float32
NT = (((1,), (1,)), ((), ()))
TN = (((0,), (0,)), ((), ()))


def each(count, step):
    if count <= 4:
        for at in range(count):
            step(at)
    else:
        lax.fori_loop(0, count, lambda at, carry: (step(at), carry)[1], 0)


def route_tables(routes, scores, groups):
    tokens = routes.shape[1]
    weight = 2.5 * scores / jnp.sum(scores, axis=0, keepdims=True)
    earlier = lax.broadcasted_iota(jnp.int32, (tokens, tokens), 0)
    later = lax.broadcasted_iota(jnp.int32, (tokens, tokens), 1)
    order = (earlier < later).astype(F32)
    rows = CAP * SUB
    slot = (lax.broadcasted_iota(jnp.int32, (rows, tokens), 0) // SUB).astype(F32)
    placed, weighted = [], []
    for group in range(groups):
        match = (routes == group).astype(F32)
        hits = jnp.broadcast_to(jnp.sum(match, axis=0, keepdims=True), (rows, tokens))
        shares = jnp.broadcast_to(jnp.sum(match * weight, axis=0, keepdims=True), (rows, tokens))
        before = jnp.dot(hits, order, preferred_element_type=F32)
        here = hits * (before == slot).astype(F32)
        placed.append(here)
        weighted.append(here * shares)
    return placed, weighted


def masks(lanes):
    part = lax.broadcasted_iota(jnp.int32, (CAP * SUB, lanes), 0) & (SUB - 1)
    return [part == at for at in range(SUB)]


def masked(held, mask):
    blocks, rows, lanes = held.shape
    return jnp.where(mask[None], held, jnp.zeros_like(held)).reshape(blocks * rows, lanes)


def kernel(
    axes, groups, lane_chunks,
    x_hbm, dy_hbm, rf_hbm, rb_hbm, sf_hbm, sb_hbm, saved_hbm, wg_hbm, wu_hbm, wd_hbm,
    out_hbm,
    tokens_s, route_s, score_s, saved_s, wgu_s, wd_s,
    saved_in, slots, shifted, total_s, total_in, rows, hid, grad, parts_s, away, mine, pair_in, pair_out, final_in, table_s, table_in, routed_s, out_s,
    load_sem, out_sem, z_send, z_recv, y_send, y_recv, a_send, a_recv, f_send, f_recv, t_send, t_recv, s_send, s_recv, x_send, x_recv,
):
    sections, ep = axes
    high = ep // PAIR
    per_group = SPLIT // PAIR
    width = slots.shape[-1]
    count = x_hbm.shape[0]
    hidden = wd_s.shape[0] // SUB
    p = lax.axis_index("pp")
    e = lax.axis_index("ep")
    hi, lo = e // PAIR, lax.rem(e, PAIR)
    other = 1 - lo
    after, before = lax.rem(p + 1, sections), lax.rem(p + sections - 1, sections)
    ahead = (after, before)

    def columns(part):
        return pl.ds(part * width, width)

    small = [
        pltpu.make_async_copy(rf_hbm, route_s.at[0], load_sem.at[0]),
        pltpu.make_async_copy(rb_hbm, route_s.at[1], load_sem.at[1]),
        pltpu.make_async_copy(sf_hbm, score_s.at[0], load_sem.at[2]),
        pltpu.make_async_copy(sb_hbm, score_s.at[1], load_sem.at[3]),
    ]
    inputs = [
        [
            pltpu.make_async_copy(
                hbm.at[:, columns(part)], tokens_s.at[d, pl.ds(part * count, count)],
                load_sem.at[4 + d * SUB + part],
            )
            for part in range(SUB)
        ]
        for d, hbm in enumerate((x_hbm, dy_hbm))
    ]
    first = 4 + 2 * SUB
    saved_load = [pltpu.make_async_copy(saved_hbm, saved_s, load_sem.at[first + 3 * SUB])]
    up_loads = [
        pltpu.make_async_copy(
            hbm.at[columns(part), :],
            wgu_s.at[:, pl.ds((2 * part + side) * hidden, hidden)],
            load_sem.at[first + side * SUB + part],
        )
        for part in range(SUB)
        for side, hbm in enumerate((wg_hbm, wu_hbm))
    ]
    down_loads = [
        pltpu.make_async_copy(
            wd_hbm.at[:, columns(part)], wd_s.at[pl.ds(part * hidden, hidden)],
            load_sem.at[first + 2 * SUB + part],
        )
        for part in range(SUB)
    ]
    for load in small + inputs[0]:
        load.start()

    barrier = pltpu.get_barrier_semaphore()

    def greet(section, at):
        pl.semaphore_signal(barrier, inc=1, device_id=(section, at), device_id_type=MESH)

    greet(p, hi * PAIR + other)
    each(high - 1, lambda k: greet(p, lax.rem(hi + k + 1, high) * PAIR + lo))
    greet(after, e)
    greet(before, e)

    for load in inputs[1]:
        load.start()

    for load in small:
        load.wait()
    tables = [route_tables(route_s[d], score_s[d], groups) for d in range(2)]
    block_rows = CAP * SUB
    for d in range(2):
        for group in range(groups):
            table_s[d, pl.ds(group * block_rows, block_rows), :] = tables[d][1][group]

    def z_copy(d, k):
        to = lax.rem(hi + k, high)
        source = shifted if d else slots.at[0]
        return pltpu.make_async_remote_copy(
            source.at[to // per_group], rows.at[d, hi, lo],
            z_send.at[d, k], z_recv.at[d, k], (p, to * PAIR + lo), MESH,
        )

    def y_copy(d, k, side):
        block = lax.rem(hi + high - k, high)
        return pltpu.make_async_remote_copy(
            rows.at[d, block, side], rows.at[d, block, side],
            y_send.at[d, k], y_recv.at[d, k], (p, hi * PAIR + other), MESH,
        )

    shift_copy = pltpu.make_async_remote_copy(
        slots.at[1], shifted, x_send.at[1], x_recv.at[1], (before, e), MESH
    )
    total_copy = pltpu.make_async_remote_copy(
        total_s, total_in, x_send.at[0], x_recv.at[0], (after, e), MESH
    )
    saved_copy = pltpu.make_async_remote_copy(saved_s, saved_in, s_send, s_recv, (before, e), MESH)

    def t_copy(d):
        return pltpu.make_async_remote_copy(
            table_s.at[d], table_in.at[d], t_send.at[d], t_recv.at[d], (ahead[d], e), MESH
        )

    lanes = SUB * count
    own_part = lax.broadcasted_iota(jnp.int32, (block_rows, lanes), 0) & (SUB - 1)
    same_part = own_part == lax.broadcasted_iota(jnp.int32, (block_rows, lanes), 1) // count

    def pick(d):
        chosen = []
        for group in range(groups):
            wide = jnp.concatenate([tables[d][0][group]] * SUB, axis=1)
            chosen.append(jnp.where(same_part, wide, 0.0).astype(BF))
        for load in inputs[d]:
            load.wait()
        for group in range(groups):
            slots[d, group] = jnp.dot(
                chosen[group], tokens_s[d], preferred_element_type=F32
            ).astype(BF)

    pick(0)
    pick(1)
    rows[0, hi, lo] = slots[0, hi // per_group]
    pl.semaphore_wait(barrier, PAIR - 1 + high - 1 + 2)
    each(high - 1, lambda k: z_copy(0, k + 1).start())
    y_copy(0, 0, lo).start()
    shift_copy.start()
    for load in saved_load + up_loads + down_loads:
        load.start()

    def relay(d):
        def step(k):
            z_copy(d, k + 1).wait_recv()
            y_copy(d, k + 1, lo).start()
        each(high - 1, step)

    def gathered(d):
        each(high, lambda k: y_copy(d, k, other).wait_recv())

    step_high = min(high, 4)
    chunks = high // step_high
    blocks = step_high * PAIR
    full = blocks * block_rows
    half = step_high * block_rows

    def spread(value):
        size, wide = value.shape
        summed = jnp.sum(value.reshape(size // SUB, SUB, wide), axis=1, keepdims=True)
        return jnp.broadcast_to(summed, (size // SUB, SUB, wide)).reshape(size, wide)

    def at_chunk(chunk):
        return pl.ds(chunk * step_high, step_high)

    def forward_hidden(chunk):
        held = rows[0, at_chunk(chunk)].reshape(blocks, block_rows, width)
        acc = jnp.zeros((full, 2 * hidden), F32)
        for part, mask in enumerate(masks(width)):
            acc += jnp.dot(
                masked(held, mask), wgu_s[:, pl.ds(part * 2 * hidden, 2 * hidden)],
                preferred_element_type=F32,
            )
        pre = spread(acc)
        gate, up = pre[:, :hidden], pre[:, hidden:]
        value = (gate / (1.0 + jnp.exp(-gate)) * up).astype(BF)
        hid[at_chunk(chunk)] = value.reshape(step_high, PAIR, block_rows, hidden)

    def backward_hidden(chunk):
        held = rows[1, at_chunk(chunk)].reshape(blocks, block_rows, width)
        acc = jnp.zeros((full, hidden), F32)
        for part, mask in enumerate(masks(width)):
            acc += lax.dot_general(
                masked(held, mask), wd_s[pl.ds(part * hidden, hidden), :], NT,
                preferred_element_type=F32,
            )
        grad_hidden = spread(acc)
        size = step_high * PAIR * CAP
        kept = saved_in[pl.ds(chunk * size, size)]
        gate = jnp.broadcast_to(kept[:, 0:1, :], (size, SUB, hidden)).reshape(full, hidden)
        up = jnp.broadcast_to(kept[:, 1:2, :], (size, SUB, hidden)).reshape(full, hidden)
        sigma = 1.0 / (1.0 + jnp.exp(-gate))
        grad_gate = (grad_hidden * up * sigma * (1.0 + gate * (1.0 - sigma))).astype(BF)
        grad_up = (grad_hidden * gate * sigma).astype(BF)
        both = jnp.concatenate([grad_gate, grad_up], axis=1)
        grad[at_chunk(chunk)] = both.reshape(step_high, PAIR, block_rows, 2 * hidden)

    def side_parts(source, chunk):
        held = jnp.concatenate([source[at_chunk(chunk), other], source[at_chunk(chunk), lo]], axis=0)
        wide = held.shape[-1]
        for part, mask in enumerate(masks(wide)):
            parts_s[pl.ds(chunk * full, full), pl.ds(part * wide, wide)] = masked(held, mask)

    def forward_out(chunk, cut):
        held = parts_s[pl.ds(chunk * full, full), pl.ds(0, SUB * hidden)]
        return jnp.dot(held, wd_s[:, cut], preferred_element_type=F32)

    def backward_out(chunk, cut):
        held = parts_s[pl.ds(chunk * full, full), :]
        return lax.dot_general(held, wgu_s[cut, :], NT, preferred_element_type=F32)

    outs = (forward_out, backward_out)
    cuts = [pl.ds(low, size) for low, size in lane_chunks]

    def a_copy(d, n):
        return pltpu.make_async_remote_copy(
            away.at[d, :, :, cuts[n]], pair_in.at[d, :, :, cuts[n]],
            a_send.at[d, n], a_recv.at[d, n], (p, hi * PAIR + other), MESH,
        )

    def f_copy(d, n, k, arriving=False):
        block = lax.rem(hi + (high - k if arriving else k), high)
        slot = block if arriving else hi
        return pltpu.make_async_remote_copy(
            pair_out.at[d, block, :, cuts[n]], final_in.at[d, slot, :, cuts[n]],
            f_send.at[d, n, k], f_recv.at[d, n, k], (p, block * PAIR + lo), MESH,
        )

    def partial(d):
        each(chunks, lambda chunk: side_parts((hid, grad)[d], chunk))
        for n, cut in enumerate(cuts):
            def make(chunk, cut=cut):
                value = outs[d](chunk, cut)
                shape = (step_high, block_rows, value.shape[1])
                away[d, at_chunk(chunk), :, cut] = value[:half].astype(BF).reshape(shape)
                mine[d, at_chunk(chunk), :, cut] = value[half:].reshape(shape)
            each(chunks, make)
            a_copy(d, n).start()

    def pass_on(d):
        for n, cut in enumerate(cuts):
            a_copy(d, n).wait_recv()

            def add(block, cut=cut):
                return (mine[d, block, :, cut] + pair_in[d, block, :, cut].astype(F32)).astype(BF)

            def send(k, n=n, cut=cut):
                block = lax.rem(hi + k + 1, high)
                pair_out[d, block, :, cut] = add(block)
                f_copy(d, n, k + 1).start()
            each(high - 1, send)
            final_in[d, hi, :, cut] = add(hi)

    def route_columns(d):
        t_copy(d).wait_recv()
        size = table_in.shape[1]
        row = lax.broadcasted_iota(jnp.int32, (size, size), 0)
        col = lax.broadcasted_iota(jnp.int32, (size, size), 1)
        return lax.dot_general(
            table_in[d], (row == col).astype(F32), TN,
            precision=lax.Precision.HIGHEST, preferred_element_type=F32,
        )

    def total(d):
        for n in range(len(cuts)):
            each(high - 1, lambda k, n=n: f_copy(d, n, k + 1, True).wait_recv())
        sums = []
        for group in range(groups):
            acc = final_in[d, group * per_group].astype(F32)
            for at in range(1, per_group):
                acc += final_in[d, group * per_group + at].astype(F32)
            sums.append(acc)
        return sums

    def finish(d, table, totals):
        for part in range(SUB):
            acc = None
            for group in range(groups):
                for slot in range(CAP):
                    at = slot * SUB + part
                    column = group * block_rows + slot * SUB
                    term = table[:, column:column + 1] * totals[group][at:at + 1, :]
                    acc = term if acc is None else acc + term
            routed = acc.astype(BF)
            if d == 0:
                routed_s[:, columns(part)] = routed
            else:
                out_s[:, columns(part)] = (
                    routed_s[:, columns(part)].astype(F32) + routed.astype(F32)
                ).astype(BF)
                out_copy(part).start()

    def out_copy(part):
        return pltpu.make_async_copy(
            out_s.at[:, columns(part)], out_hbm.at[:, columns(part)], out_sem.at[part]
        )

    relay(0)
    shift_copy.wait_recv()
    rows[1, hi, lo] = shifted[hi // per_group]
    each(high - 1, lambda k: z_copy(1, k + 1).start())
    y_copy(1, 0, lo).start()
    for load in saved_load:
        load.wait()
    saved_copy.start()
    for d in range(2):
        t_copy(d).start()
    for load in up_loads:
        load.wait()
    gathered(0)
    each(chunks, forward_hidden)
    relay(1)
    for load in down_loads:
        load.wait()
    partial(0)
    gathered(1)
    saved_copy.wait_recv()
    each(chunks, backward_hidden)
    pass_on(0)
    partial(1)
    table_f, table_b = route_columns(0), route_columns(1)
    for group, value in enumerate(total(0)):
        total_s[pl.ds(group * block_rows, block_rows), :] = value
    total_copy.start()
    pass_on(1)
    total_copy.wait_recv()
    finish(0, table_f, [total_in[pl.ds(group * block_rows, block_rows), :] for group in range(groups)])
    finish(1, table_b, total(1))

    for d in range(2):
        t_copy(d).wait_send()
        each(high - 1, lambda k, d=d: z_copy(d, k + 1).wait_send())
        each(high, lambda k, d=d: y_copy(d, k, lo).wait_send())
        for n in range(len(cuts)):
            a_copy(d, n).wait_send()
            each(high - 1, lambda k, d=d, n=n: f_copy(d, n, k + 1).wait_send())
    for copy in (saved_copy, shift_copy, total_copy):
        copy.wait_send()
    for part in range(SUB):
        out_copy(part).wait()


def write_kernel(value_hbm, out_hbm, held, load_sem, store_sem):
    wide = value_hbm.shape[1] // SUB
    loads, stores = [], []
    for at in range(SUB):
        place = (slice(None), pl.ds(at * wide, wide))
        loads.append(pltpu.make_async_copy(value_hbm.at[place], held.at[at], load_sem.at[at]))
        stores.append(pltpu.make_async_copy(held.at[at], out_hbm.at[place], store_sem.at[at]))
        loads[at].start()
    for at in range(SUB):
        loads[at].wait()
        stores[at].start()
    for store in stores:
        store.wait()


def solution(mesh):
    sections, ep = mesh.shape["pp"], mesh.shape["ep"]
    groups = ep // SPLIT
    high = ep // PAIR

    def body(x, dy, rf, rb, sf, sb, saved, wg, wu, wd):
        _, tokens, model = x.shape
        topk = rf.shape[2]
        hidden = wg.shape[1]
        width = model // SUB
        block_rows = CAP * SUB
        lane_chunks = [(low, min(512, width - low)) for low in range(0, width, 512)]
        cuts = len(lane_chunks)
        anywhere = pl.BlockSpec(memory_space=pl.ANY)
        out = pl.pallas_call(
            functools.partial(kernel, (sections, ep), groups, lane_chunks),
            out_shape=jax.ShapeDtypeStruct((tokens, model), BF),
            in_specs=[anywhere] * 10,
            out_specs=anywhere,
            scratch_shapes=[
                pltpu.VMEM((2, SUB * tokens, width), BF),
                pltpu.VMEM((2, topk, tokens), jnp.int32),
                pltpu.VMEM((2, topk, tokens), F32),
                pltpu.VMEM((ep * CAP, 2, hidden), F32),
                pltpu.VMEM((width, SUB * 2 * hidden), BF),
                pltpu.VMEM((SUB * hidden, width), BF),
                pltpu.VMEM((ep * CAP, 2, hidden), F32),
                pltpu.VMEM((2, groups, block_rows, width), BF),
                pltpu.VMEM((groups, block_rows, width), BF),
                pltpu.VMEM((groups * block_rows, width), F32),
                pltpu.VMEM((groups * block_rows, width), F32),
                pltpu.VMEM((2, high, PAIR, block_rows, width), BF),
                pltpu.VMEM((high, PAIR, block_rows, hidden), BF),
                pltpu.VMEM((high, PAIR, block_rows, 2 * hidden), BF),
                pltpu.VMEM((ep * block_rows, SUB * 2 * hidden), BF),
                pltpu.VMEM((2, high, block_rows, width), BF),
                pltpu.VMEM((2, high, block_rows, width), F32),
                pltpu.VMEM((2, high, block_rows, width), BF),
                pltpu.VMEM((2, high, block_rows, width), BF),
                pltpu.VMEM((2, high, block_rows, width), BF),
                pltpu.VMEM((2, groups * block_rows, tokens), F32),
                pltpu.VMEM((2, groups * block_rows, tokens), F32),
                pltpu.VMEM((tokens, model), BF),
                pltpu.VMEM((tokens, model), BF),
                pltpu.SemaphoreType.DMA((5 + 5 * SUB,)),
                pltpu.SemaphoreType.DMA((SUB,)),
            ]
            + [pltpu.SemaphoreType.DMA((2, high))] * 4
            + [pltpu.SemaphoreType.DMA((2, cuts))] * 2
            + [pltpu.SemaphoreType.DMA((2, cuts, high))] * 2
            + [pltpu.SemaphoreType.DMA((2,))] * 2
            + [pltpu.SemaphoreType.DMA] * 2
            + [pltpu.SemaphoreType.DMA((2,))] * 2,
            compiler_params=pltpu.CompilerParams(
                collective_id=0, has_side_effects=True, vmem_limit_bytes=VMEM_BYTES
            ),
            name="experts",
        )(
            x[0], dy[0], rf[0].T, rb[0].T, sf[0].T, sb[0].T,
            saved.reshape(ep * CAP, 2, hidden), wg, wu, wd,
        )
        out = pl.pallas_call(
            write_kernel,
            out_shape=jax.ShapeDtypeStruct((tokens, model), BF),
            in_specs=[anywhere],
            out_specs=anywhere,
            scratch_shapes=[
                pltpu.VMEM((SUB, tokens, width), BF),
                pltpu.SemaphoreType.DMA((SUB,)),
                pltpu.SemaphoreType.DMA((SUB,)),
            ],
            compiler_params=pltpu.CompilerParams(vmem_limit_bytes=VMEM_BYTES),
            name="write",
        )(out)
        return out[None]

    in_specs = (
        P("pp", "ep", None),
        P("pp", "ep", None),
        P("pp", "ep", None),
        P("pp", "ep", None),
        P("pp", "ep", None),
        P("pp", "ep", None),
        P("pp", None, None, None, "ep"),
        P(None, "ep"),
        P(None, "ep"),
        P("ep", None),
    )
    out_specs = P("pp", "ep", None)
    return jax.shard_map(body, mesh=mesh, in_specs=in_specs, out_specs=out_specs, check_vma=False)
```

```python
import functools

import jax
import jax.numpy as jnp
from jax import lax
from jax.experimental import pallas as pl
from jax.experimental.pallas import tpu as pltpu
from jax.sharding import PartitionSpec as P

SPLIT = 8
CAP = 2
SUB = 8
PAIR = 2
VMEM_BYTES = 60 * 1024 * 1024
MESH = pl.DeviceIdType.MESH
BF = jnp.bfloat16
F32 = jnp.float32
NT = (((1,), (1,)), ((), ()))
TN = (((0,), (0,)), ((), ()))


def each(count, step):
    if count <= 4:
        for at in range(count):
            step(at)
    else:
        lax.fori_loop(0, count, lambda at, carry: (step(at), carry)[1], 0)


def route_tables(routes, scores, groups):
    tokens = routes.shape[1]
    weight = 2.5 * scores / jnp.sum(scores, axis=0, keepdims=True)
    earlier = lax.broadcasted_iota(jnp.int32, (tokens, tokens), 0)
    later = lax.broadcasted_iota(jnp.int32, (tokens, tokens), 1)
    order = (earlier < later).astype(F32)
    rows = CAP * SUB
    slot = (lax.broadcasted_iota(jnp.int32, (rows, tokens), 0) // SUB).astype(F32)
    placed, weighted = [], []
    for group in range(groups):
        match = (routes == group).astype(F32)
        hits = jnp.broadcast_to(jnp.sum(match, axis=0, keepdims=True), (rows, tokens))
        shares = jnp.broadcast_to(jnp.sum(match * weight, axis=0, keepdims=True), (rows, tokens))
        before = jnp.dot(hits, order, preferred_element_type=F32)
        here = hits * (before == slot).astype(F32)
        placed.append(here)
        weighted.append(here * shares)
    return placed, weighted


def masks(lanes):
    part = lax.broadcasted_iota(jnp.int32, (CAP * SUB, lanes), 0) & (SUB - 1)
    return [part == at for at in range(SUB)]


def masked(held, mask):
    blocks, rows, lanes = held.shape
    return jnp.where(mask[None], held, jnp.zeros_like(held)).reshape(blocks * rows, lanes)


def kernel(
    axes, groups, lane_chunks,
    x_hbm, dy_hbm, rf_hbm, rb_hbm, sf_hbm, sb_hbm, saved_hbm, wg_hbm, wu_hbm, wd_hbm,
    out_hbm,
    tokens_s, route_s, score_s, saved_s, wgu_s, wd_s,
    saved_in, slots, shifted, total_s, total_in, rows, hid, grad, parts_s, away, mine, pair_in, pair_out, final_in, table_s, table_in, routed_s, out_s,
    load_sem, out_sem, z_send, z_recv, y_send, y_recv, a_send, a_recv, f_send, f_recv, t_send, t_recv, s_send, s_recv, x_send, x_recv,
):
    sections, ep = axes
    high = ep // PAIR
    per_group = SPLIT // PAIR
    width = slots.shape[-1]
    count = x_hbm.shape[0]
    hidden = wd_s.shape[0] // SUB
    p = lax.axis_index("pp")
    e = lax.axis_index("ep")
    hi, lo = e // PAIR, lax.rem(e, PAIR)
    other = 1 - lo
    after, before = lax.rem(p + 1, sections), lax.rem(p + sections - 1, sections)
    ahead = (after, before)

    def columns(part):
        return pl.ds(part * width, width)

    small = [
        pltpu.make_async_copy(rf_hbm, route_s.at[0], load_sem.at[0]),
        pltpu.make_async_copy(rb_hbm, route_s.at[1], load_sem.at[1]),
        pltpu.make_async_copy(sf_hbm, score_s.at[0], load_sem.at[2]),
        pltpu.make_async_copy(sb_hbm, score_s.at[1], load_sem.at[3]),
    ]
    inputs = [
        [
            pltpu.make_async_copy(
                hbm.at[:, columns(part)], tokens_s.at[d, pl.ds(part * count, count)],
                load_sem.at[4 + d * SUB + part],
            )
            for part in range(SUB)
        ]
        for d, hbm in enumerate((x_hbm, dy_hbm))
    ]
    first = 4 + 2 * SUB
    saved_load = [pltpu.make_async_copy(saved_hbm, saved_s, load_sem.at[first + 3 * SUB])]
    up_loads = [
        pltpu.make_async_copy(
            hbm.at[columns(part), :],
            wgu_s.at[:, pl.ds((2 * part + side) * hidden, hidden)],
            load_sem.at[first + side * SUB + part],
        )
        for part in range(SUB)
        for side, hbm in enumerate((wg_hbm, wu_hbm))
    ]
    down_loads = [
        pltpu.make_async_copy(
            wd_hbm.at[:, columns(part)], wd_s.at[pl.ds(part * hidden, hidden)],
            load_sem.at[first + 2 * SUB + part],
        )
        for part in range(SUB)
    ]
    for load in small + inputs[0]:
        load.start()

    barrier = pltpu.get_barrier_semaphore()

    def greet(section, at):
        pl.semaphore_signal(barrier, inc=1, device_id=(section, at), device_id_type=MESH)

    greet(p, hi * PAIR + other)
    each(high - 1, lambda k: greet(p, lax.rem(hi + k + 1, high) * PAIR + lo))
    greet(after, e)
    greet(before, e)

    for load in inputs[1]:
        load.start()

    for load in small:
        load.wait()
    tables = [route_tables(route_s[d], score_s[d], groups) for d in range(2)]
    block_rows = CAP * SUB
    for d in range(2):
        for group in range(groups):
            table_s[d, pl.ds(group * block_rows, block_rows), :] = tables[d][1][group]

    def z_copy(d, k):
        to = lax.rem(hi + k, high)
        source = shifted if d else slots.at[0]
        return pltpu.make_async_remote_copy(
            source.at[to // per_group], rows.at[d, hi, lo],
            z_send.at[d, k], z_recv.at[d, k], (p, to * PAIR + lo), MESH,
        )

    def y_copy(d, k, side):
        block = lax.rem(hi + high - k, high)
        return pltpu.make_async_remote_copy(
            rows.at[d, block, side], rows.at[d, block, side],
            y_send.at[d, k], y_recv.at[d, k], (p, hi * PAIR + other), MESH,
        )

    shift_copy = pltpu.make_async_remote_copy(
        slots.at[1], shifted, x_send.at[1], x_recv.at[1], (before, e), MESH
    )
    total_copy = pltpu.make_async_remote_copy(
        total_s, total_in, x_send.at[0], x_recv.at[0], (after, e), MESH
    )
    saved_copy = pltpu.make_async_remote_copy(saved_s, saved_in, s_send, s_recv, (before, e), MESH)

    def t_copy(d):
        return pltpu.make_async_remote_copy(
            table_s.at[d], table_in.at[d], t_send.at[d], t_recv.at[d], (ahead[d], e), MESH
        )

    lanes = SUB * count
    own_part = lax.broadcasted_iota(jnp.int32, (block_rows, lanes), 0) & (SUB - 1)
    same_part = own_part == lax.broadcasted_iota(jnp.int32, (block_rows, lanes), 1) // count

    def pick(d):
        chosen = []
        for group in range(groups):
            wide = jnp.concatenate([tables[d][0][group]] * SUB, axis=1)
            chosen.append(jnp.where(same_part, wide, 0.0).astype(BF))
        for load in inputs[d]:
            load.wait()
        for group in range(groups):
            slots[d, group] = jnp.dot(
                chosen[group], tokens_s[d], preferred_element_type=F32
            ).astype(BF)

    pick(0)
    pick(1)
    rows[0, hi, lo] = slots[0, hi // per_group]
    pl.semaphore_wait(barrier, PAIR - 1 + high - 1 + 2)
    each(high - 1, lambda k: z_copy(0, k + 1).start())
    y_copy(0, 0, lo).start()
    shift_copy.start()
    for load in saved_load + up_loads + down_loads:
        load.start()

    def relay(d):
        def step(k):
            z_copy(d, k + 1).wait_recv()
            y_copy(d, k + 1, lo).start()
        each(high - 1, step)

    def gathered(d):
        each(high, lambda k: y_copy(d, k, other).wait_recv())

    step_high = min(high, 4)
    chunks = high // step_high
    blocks = step_high * PAIR
    full = blocks * block_rows
    half = step_high * block_rows

    def spread(value):
        size, wide = value.shape
        summed = jnp.sum(value.reshape(size // SUB, SUB, wide), axis=1, keepdims=True)
        return jnp.broadcast_to(summed, (size // SUB, SUB, wide)).reshape(size, wide)

    def at_chunk(chunk):
        return pl.ds(chunk * step_high, step_high)

    def forward_hidden(chunk):
        held = rows[0, at_chunk(chunk)].reshape(blocks, block_rows, width)
        acc = jnp.zeros((full, 2 * hidden), F32)
        for part, mask in enumerate(masks(width)):
            acc += jnp.dot(
                masked(held, mask), wgu_s[:, pl.ds(part * 2 * hidden, 2 * hidden)],
                preferred_element_type=F32,
            )
        pre = spread(acc)
        gate, up = pre[:, :hidden], pre[:, hidden:]
        value = (gate / (1.0 + jnp.exp(-gate)) * up).astype(BF)
        hid[at_chunk(chunk)] = value.reshape(step_high, PAIR, block_rows, hidden)

    def backward_hidden(chunk):
        held = rows[1, at_chunk(chunk)].reshape(blocks, block_rows, width)
        acc = jnp.zeros((full, hidden), F32)
        for part, mask in enumerate(masks(width)):
            acc += lax.dot_general(
                masked(held, mask), wd_s[pl.ds(part * hidden, hidden), :], NT,
                preferred_element_type=F32,
            )
        grad_hidden = spread(acc)
        size = step_high * PAIR * CAP
        kept = saved_in[pl.ds(chunk * size, size)]
        gate = jnp.broadcast_to(kept[:, 0:1, :], (size, SUB, hidden)).reshape(full, hidden)
        up = jnp.broadcast_to(kept[:, 1:2, :], (size, SUB, hidden)).reshape(full, hidden)
        sigma = 1.0 / (1.0 + jnp.exp(-gate))
        grad_gate = (grad_hidden * up * sigma * (1.0 + gate * (1.0 - sigma))).astype(BF)
        grad_up = (grad_hidden * gate * sigma).astype(BF)
        both = jnp.concatenate([grad_gate, grad_up], axis=1)
        grad[at_chunk(chunk)] = both.reshape(step_high, PAIR, block_rows, 2 * hidden)

    def side_parts(source, chunk):
        held = jnp.concatenate([source[at_chunk(chunk), other], source[at_chunk(chunk), lo]], axis=0)
        wide = held.shape[-1]
        for part, mask in enumerate(masks(wide)):
            parts_s[pl.ds(chunk * full, full), pl.ds(part * wide, wide)] = masked(held, mask)

    def forward_out(chunk, cut):
        held = parts_s[pl.ds(chunk * full, full), pl.ds(0, SUB * hidden)]
        return jnp.dot(held, wd_s[:, cut], preferred_element_type=F32)

    def backward_out(chunk, cut):
        held = parts_s[pl.ds(chunk * full, full), :]
        return lax.dot_general(held, wgu_s[cut, :], NT, preferred_element_type=F32)

    outs = (forward_out, backward_out)
    cuts = [pl.ds(low, size) for low, size in lane_chunks]

    def a_copy(d, n):
        return pltpu.make_async_remote_copy(
            away.at[d, :, :, cuts[n]], pair_in.at[d, :, :, cuts[n]],
            a_send.at[d, n], a_recv.at[d, n], (p, hi * PAIR + other), MESH,
        )

    def f_copy(d, n, k, arriving=False):
        block = lax.rem(hi + (high - k if arriving else k), high)
        slot = block if arriving else hi
        return pltpu.make_async_remote_copy(
            pair_out.at[d, block, :, cuts[n]], final_in.at[d, slot, :, cuts[n]],
            f_send.at[d, n, k], f_recv.at[d, n, k], (p, block * PAIR + lo), MESH,
        )

    def partial(d):
        each(chunks, lambda chunk: side_parts((hid, grad)[d], chunk))
        for n, cut in enumerate(cuts):
            def make(chunk, cut=cut):
                value = outs[d](chunk, cut)
                shape = (step_high, block_rows, value.shape[1])
                away[d, at_chunk(chunk), :, cut] = value[:half].astype(BF).reshape(shape)
                mine[d, at_chunk(chunk), :, cut] = value[half:].reshape(shape)
            each(chunks, make)
            a_copy(d, n).start()

    def pass_on(d):
        for n, cut in enumerate(cuts):
            a_copy(d, n).wait_recv()

            def add(block, cut=cut):
                return (mine[d, block, :, cut] + pair_in[d, block, :, cut].astype(F32)).astype(BF)

            def send(k, n=n, cut=cut):
                block = lax.rem(hi + k + 1, high)
                pair_out[d, block, :, cut] = add(block)
                f_copy(d, n, k + 1).start()
            each(high - 1, send)
            final_in[d, hi, :, cut] = add(hi)

    def route_columns(d):
        t_copy(d).wait_recv()
        size = table_in.shape[1]
        row = lax.broadcasted_iota(jnp.int32, (size, size), 0)
        col = lax.broadcasted_iota(jnp.int32, (size, size), 1)
        return lax.dot_general(
            table_in[d], (row == col).astype(F32), TN,
            precision=lax.Precision.HIGHEST, preferred_element_type=F32,
        )

    def total(d):
        for n in range(len(cuts)):
            each(high - 1, lambda k, n=n: f_copy(d, n, k + 1, True).wait_recv())
        sums = []
        for group in range(groups):
            acc = final_in[d, group * per_group].astype(F32)
            for at in range(1, per_group):
                acc += final_in[d, group * per_group + at].astype(F32)
            sums.append(acc)
        return sums

    def finish(d, table, totals):
        for part in range(SUB):
            acc = None
            for group in range(groups):
                for slot in range(CAP):
                    at = slot * SUB + part
                    column = group * block_rows + slot * SUB
                    term = table[:, column:column + 1] * totals[group][at:at + 1, :]
                    acc = term if acc is None else acc + term
            routed = acc.astype(BF)
            if d == 1:
                routed_s[:, columns(part)] = routed
            else:
                out_s[:, columns(part)] = (
                    routed_s[:, columns(part)].astype(F32) + routed.astype(F32)
                ).astype(BF)
                out_copy(part).start()

    def out_copy(part):
        return pltpu.make_async_copy(
            out_s.at[:, columns(part)], out_hbm.at[:, columns(part)], out_sem.at[part]
        )

    relay(0)
    shift_copy.wait_recv()
    rows[1, hi, lo] = shifted[hi // per_group]
    each(high - 1, lambda k: z_copy(1, k + 1).start())
    y_copy(1, 0, lo).start()
    for load in saved_load:
        load.wait()
    saved_copy.start()
    for d in range(2):
        t_copy(d).start()
    for load in up_loads:
        load.wait()
    gathered(0)
    each(chunks, forward_hidden)
    relay(1)
    for load in down_loads:
        load.wait()
    partial(0)
    gathered(1)
    saved_copy.wait_recv()
    each(chunks, backward_hidden)
    pass_on(0)
    partial(1)
    table_f, table_b = route_columns(0), route_columns(1)
    for group, value in enumerate(total(0)):
        total_s[pl.ds(group * block_rows, block_rows), :] = value.astype(BF)
    total_copy.start()
    pass_on(1)
    finish(1, table_b, total(1))
    total_copy.wait_recv()
    finish(0, table_f, [
        total_in[pl.ds(group * block_rows, block_rows), :].astype(F32) for group in range(groups)
    ])

    for d in range(2):
        t_copy(d).wait_send()
        each(high - 1, lambda k, d=d: z_copy(d, k + 1).wait_send())
        each(high, lambda k, d=d: y_copy(d, k, lo).wait_send())
        for n in range(len(cuts)):
            a_copy(d, n).wait_send()
            each(high - 1, lambda k, d=d, n=n: f_copy(d, n, k + 1).wait_send())
    for copy in (saved_copy, shift_copy, total_copy):
        copy.wait_send()
    for part in range(SUB):
        out_copy(part).wait()


def write_kernel(value_hbm, out_hbm, held, load_sem, store_sem):
    wide = value_hbm.shape[1] // SUB
    loads, stores = [], []
    for at in range(SUB):
        place = (slice(None), pl.ds(at * wide, wide))
        loads.append(pltpu.make_async_copy(value_hbm.at[place], held.at[at], load_sem.at[at]))
        stores.append(pltpu.make_async_copy(held.at[at], out_hbm.at[place], store_sem.at[at]))
        loads[at].start()
    for at in range(SUB):
        loads[at].wait()
        stores[at].start()
    for store in stores:
        store.wait()


def solution(mesh):
    sections, ep = mesh.shape["pp"], mesh.shape["ep"]
    groups = ep // SPLIT
    high = ep // PAIR

    def body(x, dy, rf, rb, sf, sb, saved, wg, wu, wd):
        _, tokens, model = x.shape
        topk = rf.shape[2]
        hidden = wg.shape[1]
        width = model // SUB
        block_rows = CAP * SUB
        lane_chunks = [(low, min(512, width - low)) for low in range(0, width, 512)]
        cuts = len(lane_chunks)
        anywhere = pl.BlockSpec(memory_space=pl.ANY)
        out = pl.pallas_call(
            functools.partial(kernel, (sections, ep), groups, lane_chunks),
            out_shape=jax.ShapeDtypeStruct((tokens, model), BF),
            in_specs=[anywhere] * 10,
            out_specs=anywhere,
            scratch_shapes=[
                pltpu.VMEM((2, SUB * tokens, width), BF),
                pltpu.VMEM((2, topk, tokens), jnp.int32),
                pltpu.VMEM((2, topk, tokens), F32),
                pltpu.VMEM((ep * CAP, 2, hidden), F32),
                pltpu.VMEM((width, SUB * 2 * hidden), BF),
                pltpu.VMEM((SUB * hidden, width), BF),
                pltpu.VMEM((ep * CAP, 2, hidden), F32),
                pltpu.VMEM((2, groups, block_rows, width), BF),
                pltpu.VMEM((groups, block_rows, width), BF),
                pltpu.VMEM((groups * block_rows, width), BF),
                pltpu.VMEM((groups * block_rows, width), BF),
                pltpu.VMEM((2, high, PAIR, block_rows, width), BF),
                pltpu.VMEM((high, PAIR, block_rows, hidden), BF),
                pltpu.VMEM((high, PAIR, block_rows, 2 * hidden), BF),
                pltpu.VMEM((ep * block_rows, SUB * 2 * hidden), BF),
                pltpu.VMEM((2, high, block_rows, width), BF),
                pltpu.VMEM((2, high, block_rows, width), F32),
                pltpu.VMEM((2, high, block_rows, width), BF),
                pltpu.VMEM((2, high, block_rows, width), BF),
                pltpu.VMEM((2, high, block_rows, width), BF),
                pltpu.VMEM((2, groups * block_rows, tokens), F32),
                pltpu.VMEM((2, groups * block_rows, tokens), F32),
                pltpu.VMEM((tokens, model), BF),
                pltpu.VMEM((tokens, model), BF),
                pltpu.SemaphoreType.DMA((5 + 5 * SUB,)),
                pltpu.SemaphoreType.DMA((SUB,)),
            ]
            + [pltpu.SemaphoreType.DMA((2, high))] * 4
            + [pltpu.SemaphoreType.DMA((2, cuts))] * 2
            + [pltpu.SemaphoreType.DMA((2, cuts, high))] * 2
            + [pltpu.SemaphoreType.DMA((2,))] * 2
            + [pltpu.SemaphoreType.DMA] * 2
            + [pltpu.SemaphoreType.DMA((2,))] * 2,
            compiler_params=pltpu.CompilerParams(
                collective_id=0, has_side_effects=True, vmem_limit_bytes=VMEM_BYTES
            ),
            name="experts",
        )(
            x[0], dy[0], rf[0].T, rb[0].T, sf[0].T, sb[0].T,
            saved.reshape(ep * CAP, 2, hidden), wg, wu, wd,
        )
        out = pl.pallas_call(
            write_kernel,
            out_shape=jax.ShapeDtypeStruct((tokens, model), BF),
            in_specs=[anywhere],
            out_specs=anywhere,
            scratch_shapes=[
                pltpu.VMEM((SUB, tokens, width), BF),
                pltpu.SemaphoreType.DMA((SUB,)),
                pltpu.SemaphoreType.DMA((SUB,)),
            ],
            compiler_params=pltpu.CompilerParams(vmem_limit_bytes=VMEM_BYTES),
            name="write",
        )(out)
        return out[None]

    in_specs = (
        P("pp", "ep", None),
        P("pp", "ep", None),
        P("pp", "ep", None),
        P("pp", "ep", None),
        P("pp", "ep", None),
        P("pp", "ep", None),
        P("pp", None, None, None, "ep"),
        P(None, "ep"),
        P(None, "ep"),
        P("ep", None),
    )
    out_specs = P("pp", "ep", None)
    return jax.shard_map(body, mesh=mesh, in_specs=in_specs, out_specs=out_specs, check_vma=False)
```

```python
import functools

import jax
import jax.numpy as jnp
from jax import lax
from jax.experimental import pallas as pl
from jax.experimental.pallas import tpu as pltpu
from jax.sharding import PartitionSpec as P

SPLIT = 8
CAP = 2
SUB = 8
PAIR = 2
VMEM_BYTES = 60 * 1024 * 1024
MESH = pl.DeviceIdType.MESH
BF = jnp.bfloat16
F32 = jnp.float32
NT = (((1,), (1,)), ((), ()))
TN = (((0,), (0,)), ((), ()))


def each(count, step):
    if count <= 4:
        for at in range(count):
            step(at)
    else:
        lax.fori_loop(0, count, lambda at, carry: (step(at), carry)[1], 0)


def route_tables(routes, scores, groups):
    tokens = routes.shape[1]
    weight = 2.5 * scores / jnp.sum(scores, axis=0, keepdims=True)
    earlier = lax.broadcasted_iota(jnp.int32, (tokens, tokens), 0)
    later = lax.broadcasted_iota(jnp.int32, (tokens, tokens), 1)
    order = (earlier < later).astype(F32)
    rows = CAP * SUB
    slot = (lax.broadcasted_iota(jnp.int32, (rows, tokens), 0) // SUB).astype(F32)
    placed, weighted = [], []
    for group in range(groups):
        match = (routes == group).astype(F32)
        hits = jnp.broadcast_to(jnp.sum(match, axis=0, keepdims=True), (rows, tokens))
        shares = jnp.broadcast_to(jnp.sum(match * weight, axis=0, keepdims=True), (rows, tokens))
        before = jnp.dot(hits, order, preferred_element_type=F32)
        here = hits * (before == slot).astype(F32)
        placed.append(here)
        weighted.append(here * shares)
    return placed, weighted


def masks(lanes):
    part = lax.broadcasted_iota(jnp.int32, (CAP * SUB, lanes), 0) & (SUB - 1)
    return [part == at for at in range(SUB)]


def masked(held, mask):
    blocks, rows, lanes = held.shape
    return jnp.where(mask[None], held, jnp.zeros_like(held)).reshape(blocks * rows, lanes)


def kernel(
    axes, groups, lane_chunks,
    x_hbm, dy_hbm, rf_hbm, rb_hbm, sf_hbm, sb_hbm, saved_hbm, wg_hbm, wu_hbm, wd_hbm,
    out_hbm,
    tokens_s, route_s, score_s, saved_s, wgu_s, wd_s,
    saved_in, slots, shifted, total_s, total_in, rows, hid, grad, parts_s, away, mine, pair_in, pair_out, final_in, table_s, table_in, routed_s, out_s,
    load_sem, out_sem, z_send, z_recv, y_send, y_recv, a_send, a_recv, f_send, f_recv, t_send, t_recv, s_send, s_recv, x_send, x_recv,
):
    sections, ep = axes
    high = ep // PAIR
    per_group = SPLIT // PAIR
    width = slots.shape[-1]
    count = x_hbm.shape[0]
    hidden = wd_s.shape[0] // SUB
    p = lax.axis_index("pp")
    e = lax.axis_index("ep")
    hi, lo = e // PAIR, lax.rem(e, PAIR)
    other = 1 - lo
    after, before = lax.rem(p + 1, sections), lax.rem(p + sections - 1, sections)
    ahead = (after, before)

    def columns(part):
        return pl.ds(part * width, width)

    small = [
        pltpu.make_async_copy(rf_hbm, route_s.at[0], load_sem.at[0]),
        pltpu.make_async_copy(rb_hbm, route_s.at[1], load_sem.at[1]),
        pltpu.make_async_copy(sf_hbm, score_s.at[0], load_sem.at[2]),
        pltpu.make_async_copy(sb_hbm, score_s.at[1], load_sem.at[3]),
    ]
    inputs = [
        [
            pltpu.make_async_copy(
                hbm.at[:, columns(part)], tokens_s.at[d, pl.ds(part * count, count)],
                load_sem.at[4 + d * SUB + part],
            )
            for part in range(SUB)
        ]
        for d, hbm in enumerate((x_hbm, dy_hbm))
    ]
    first = 4 + 2 * SUB
    saved_load = [pltpu.make_async_copy(saved_hbm, saved_s, load_sem.at[first + 3 * SUB])]
    up_loads = [
        pltpu.make_async_copy(
            hbm.at[columns(part), :],
            wgu_s.at[:, pl.ds((2 * part + side) * hidden, hidden)],
            load_sem.at[first + side * SUB + part],
        )
        for part in range(SUB)
        for side, hbm in enumerate((wg_hbm, wu_hbm))
    ]
    down_loads = [
        pltpu.make_async_copy(
            wd_hbm.at[:, columns(part)], wd_s.at[pl.ds(part * hidden, hidden)],
            load_sem.at[first + 2 * SUB + part],
        )
        for part in range(SUB)
    ]
    for load in small + inputs[0]:
        load.start()

    barrier = pltpu.get_barrier_semaphore()

    def greet(section, at):
        pl.semaphore_signal(barrier, inc=1, device_id=(section, at), device_id_type=MESH)

    greet(p, hi * PAIR + other)
    each(high - 1, lambda k: greet(p, lax.rem(hi + k + 1, high) * PAIR + lo))
    greet(after, e)
    greet(before, e)

    for load in inputs[1]:
        load.start()

    for load in small:
        load.wait()
    tables = [route_tables(route_s[d], score_s[d], groups) for d in range(2)]
    block_rows = CAP * SUB
    for d in range(2):
        for group in range(groups):
            table_s[d, pl.ds(group * block_rows, block_rows), :] = tables[d][1][group]

    def z_copy(d, k):
        to = lax.rem(hi + k, high)
        source = shifted if d else slots.at[0]
        return pltpu.make_async_remote_copy(
            source.at[to // per_group], rows.at[d, hi, lo],
            z_send.at[d, k], z_recv.at[d, k], (p, to * PAIR + lo), MESH,
        )

    def y_copy(d, k, side):
        block = lax.rem(hi + high - k, high)
        return pltpu.make_async_remote_copy(
            rows.at[d, block, side], rows.at[d, block, side],
            y_send.at[d, k], y_recv.at[d, k], (p, hi * PAIR + other), MESH,
        )

    shift_copy = pltpu.make_async_remote_copy(
        slots.at[1], shifted, x_send.at[1], x_recv.at[1], (before, e), MESH
    )
    total_copy = pltpu.make_async_remote_copy(
        total_s, total_in, x_send.at[0], x_recv.at[0], (after, e), MESH
    )
    saved_copy = pltpu.make_async_remote_copy(saved_s, saved_in, s_send, s_recv, (before, e), MESH)

    def t_copy(d):
        return pltpu.make_async_remote_copy(
            table_s.at[d], table_in.at[d], t_send.at[d], t_recv.at[d], (ahead[d], e), MESH
        )

    lanes = SUB * count
    own_part = lax.broadcasted_iota(jnp.int32, (block_rows, lanes), 0) & (SUB - 1)
    same_part = own_part == lax.broadcasted_iota(jnp.int32, (block_rows, lanes), 1) // count

    def pick(d):
        chosen = []
        for group in range(groups):
            wide = jnp.concatenate([tables[d][0][group]] * SUB, axis=1)
            chosen.append(jnp.where(same_part, wide, 0.0).astype(BF))
        for load in inputs[d]:
            load.wait()
        for group in range(groups):
            slots[d, group] = jnp.dot(
                chosen[group], tokens_s[d], preferred_element_type=F32
            ).astype(BF)

    pick(0)
    pick(1)
    rows[0, hi, lo] = slots[0, hi // per_group]
    pl.semaphore_wait(barrier, PAIR - 1 + high - 1 + 2)
    each(high - 1, lambda k: z_copy(0, k + 1).start())
    y_copy(0, 0, lo).start()
    shift_copy.start()
    for load in saved_load + up_loads + down_loads:
        load.start()

    def relay(d):
        def step(k):
            z_copy(d, k + 1).wait_recv()
            y_copy(d, k + 1, lo).start()
        each(high - 1, step)

    def gathered(d):
        each(high, lambda k: y_copy(d, k, other).wait_recv())

    step_high = min(high, 4)
    chunks = high // step_high
    blocks = step_high * PAIR
    full = blocks * block_rows
    half = step_high * block_rows

    def spread(value):
        size, wide = value.shape
        summed = jnp.sum(value.reshape(size // SUB, SUB, wide), axis=1, keepdims=True)
        return jnp.broadcast_to(summed, (size // SUB, SUB, wide)).reshape(size, wide)

    def at_chunk(chunk):
        return pl.ds(chunk * step_high, step_high)

    def forward_hidden(chunk):
        held = rows[0, at_chunk(chunk)].reshape(blocks, block_rows, width)
        acc = jnp.zeros((full, 2 * hidden), F32)
        for part, mask in enumerate(masks(width)):
            acc += jnp.dot(
                masked(held, mask), wgu_s[:, pl.ds(part * 2 * hidden, 2 * hidden)],
                preferred_element_type=F32,
            )
        pre = spread(acc)
        gate, up = pre[:, :hidden], pre[:, hidden:]
        value = (gate / (1.0 + jnp.exp(-gate)) * up).astype(BF)
        hid[at_chunk(chunk)] = value.reshape(step_high, PAIR, block_rows, hidden)

    def backward_hidden(chunk):
        held = rows[1, at_chunk(chunk)].reshape(blocks, block_rows, width)
        acc = jnp.zeros((full, hidden), F32)
        for part, mask in enumerate(masks(width)):
            acc += lax.dot_general(
                masked(held, mask), wd_s[pl.ds(part * hidden, hidden), :], NT,
                preferred_element_type=F32,
            )
        grad_hidden = spread(acc)
        size = step_high * PAIR * CAP
        kept = saved_in[pl.ds(chunk * size, size)]
        gate = jnp.broadcast_to(kept[:, 0:1, :], (size, SUB, hidden)).reshape(full, hidden)
        up = jnp.broadcast_to(kept[:, 1:2, :], (size, SUB, hidden)).reshape(full, hidden)
        sigma = 1.0 / (1.0 + jnp.exp(-gate))
        grad_gate = (grad_hidden * up * sigma * (1.0 + gate * (1.0 - sigma))).astype(BF)
        grad_up = (grad_hidden * gate * sigma).astype(BF)
        both = jnp.concatenate([grad_gate, grad_up], axis=1)
        grad[at_chunk(chunk)] = both.reshape(step_high, PAIR, block_rows, 2 * hidden)

    def side_parts(source, chunk):
        held = jnp.concatenate([source[at_chunk(chunk), other], source[at_chunk(chunk), lo]], axis=0)
        wide = held.shape[-1]
        for part, mask in enumerate(masks(wide)):
            parts_s[pl.ds(chunk * full, full), pl.ds(part * wide, wide)] = masked(held, mask)

    def forward_out(chunk, cut):
        held = parts_s[pl.ds(chunk * full, full), pl.ds(0, SUB * hidden)]
        return jnp.dot(held, wd_s[:, cut], preferred_element_type=F32)

    def backward_out(chunk, cut):
        held = parts_s[pl.ds(chunk * full, full), :]
        return lax.dot_general(held, wgu_s[cut, :], NT, preferred_element_type=F32)

    outs = (forward_out, backward_out)
    cuts = [pl.ds(low, size) for low, size in lane_chunks]

    def a_copy(d, n):
        return pltpu.make_async_remote_copy(
            away.at[d, :, :, cuts[n]], pair_in.at[d, :, :, cuts[n]],
            a_send.at[d, n], a_recv.at[d, n], (p, hi * PAIR + other), MESH,
        )

    def f_copy(d, n, k, arriving=False):
        block = lax.rem(hi + (high - k if arriving else k), high)
        slot = block if arriving else hi
        return pltpu.make_async_remote_copy(
            pair_out.at[d, block, :, cuts[n]], final_in.at[d, slot, :, cuts[n]],
            f_send.at[d, n, k], f_recv.at[d, n, k], (p, block * PAIR + lo), MESH,
        )

    def partial(d):
        each(chunks, lambda chunk: side_parts((hid, grad)[d], chunk))
        for n, cut in enumerate(cuts):
            def make(chunk, cut=cut):
                value = outs[d](chunk, cut)
                shape = (step_high, block_rows, value.shape[1])
                away[d, at_chunk(chunk), :, cut] = value[:half].astype(BF).reshape(shape)
                mine[d, at_chunk(chunk), :, cut] = value[half:].reshape(shape)
            each(chunks, make)
            a_copy(d, n).start()

    def pass_on(d):
        for n, cut in enumerate(cuts):
            a_copy(d, n).wait_recv()

            def add(block, cut=cut):
                return (mine[d, block, :, cut] + pair_in[d, block, :, cut].astype(F32)).astype(BF)

            def send(k, n=n, cut=cut):
                block = lax.rem(hi + k + 1, high)
                pair_out[d, block, :, cut] = add(block)
                f_copy(d, n, k + 1).start()
            each(high - 1, send)
            final_in[d, hi, :, cut] = add(hi)

    def route_columns(d):
        t_copy(d).wait_recv()
        size = table_in.shape[1]
        row = lax.broadcasted_iota(jnp.int32, (size, size), 0)
        col = lax.broadcasted_iota(jnp.int32, (size, size), 1)
        return lax.dot_general(
            table_in[d], (row == col).astype(F32), TN,
            precision=lax.Precision.HIGHEST, preferred_element_type=F32,
        )

    def total(d):
        for n in range(len(cuts)):
            each(high - 1, lambda k, n=n: f_copy(d, n, k + 1, True).wait_recv())
        sums = []
        for group in range(groups):
            acc = final_in[d, group * per_group].astype(F32)
            for at in range(1, per_group):
                acc += final_in[d, group * per_group + at].astype(F32)
            sums.append(acc)
        return sums

    def finish(d, table, totals):
        for part in range(SUB):
            acc = None
            for group in range(groups):
                for slot in range(CAP):
                    at = slot * SUB + part
                    column = group * block_rows + slot * SUB
                    term = table[:, column:column + 1] * totals[group][at:at + 1, :]
                    acc = term if acc is None else acc + term
            routed = acc.astype(BF)
            if d == 0:
                routed_s[:, columns(part)] = routed
            else:
                out_s[:, columns(part)] = (
                    routed_s[:, columns(part)].astype(F32) + routed.astype(F32)
                ).astype(BF)
                out_copy(part).start()

    def out_copy(part):
        return pltpu.make_async_copy(
            out_s.at[:, columns(part)], out_hbm.at[:, columns(part)], out_sem.at[part]
        )

    relay(0)
    shift_copy.wait_recv()
    rows[1, hi, lo] = shifted[hi // per_group]
    each(high - 1, lambda k: z_copy(1, k + 1).start())
    y_copy(1, 0, lo).start()
    for load in saved_load:
        load.wait()
    saved_copy.start()
    for d in range(2):
        t_copy(d).start()
    for load in up_loads:
        load.wait()
    gathered(0)
    each(chunks, forward_hidden)
    relay(1)
    for load in down_loads:
        load.wait()
    partial(0)
    gathered(1)
    saved_copy.wait_recv()
    each(chunks, backward_hidden)
    pass_on(0)
    partial(1)
    table_f, table_b = route_columns(0), route_columns(1)
    for group, value in enumerate(total(0)):
        total_s[pl.ds(group * block_rows, block_rows), :] = value
    total_copy.start()
    pass_on(1)
    total_copy.wait_recv()
    finish(0, table_f, [total_in[pl.ds(group * block_rows, block_rows), :] for group in range(groups)])
    finish(1, table_b, total(1))

    for d in range(2):
        t_copy(d).wait_send()
        each(high - 1, lambda k, d=d: z_copy(d, k + 1).wait_send())
        each(high, lambda k, d=d: y_copy(d, k, lo).wait_send())
        for n in range(len(cuts)):
            a_copy(d, n).wait_send()
            each(high - 1, lambda k, d=d, n=n: f_copy(d, n, k + 1).wait_send())
    for copy in (saved_copy, shift_copy, total_copy):
        copy.wait_send()
    for part in range(SUB):
        out_copy(part).wait()


def write_kernel(value_hbm, out_hbm, held, load_sem, store_sem):
    wide = value_hbm.shape[1] // SUB
    loads, stores = [], []
    for at in range(SUB):
        place = (slice(None), pl.ds(at * wide, wide))
        loads.append(pltpu.make_async_copy(value_hbm.at[place], held.at[at], load_sem.at[at]))
        stores.append(pltpu.make_async_copy(held.at[at], out_hbm.at[place], store_sem.at[at]))
        loads[at].start()
    for at in range(SUB):
        loads[at].wait()
        stores[at].start()
    for store in stores:
        store.wait()


def solution(mesh):
    sections, ep = mesh.shape["pp"], mesh.shape["ep"]
    groups = ep // SPLIT
    high = ep // PAIR

    def body(x, dy, rf, rb, sf, sb, saved, wg, wu, wd):
        _, tokens, model = x.shape
        topk = rf.shape[2]
        hidden = wg.shape[1]
        width = model // SUB
        block_rows = CAP * SUB
        lane_chunks = [(0, width)]
        cuts = len(lane_chunks)
        anywhere = pl.BlockSpec(memory_space=pl.ANY)
        out = pl.pallas_call(
            functools.partial(kernel, (sections, ep), groups, lane_chunks),
            out_shape=jax.ShapeDtypeStruct((tokens, model), BF),
            in_specs=[anywhere] * 10,
            out_specs=anywhere,
            scratch_shapes=[
                pltpu.VMEM((2, SUB * tokens, width), BF),
                pltpu.VMEM((2, topk, tokens), jnp.int32),
                pltpu.VMEM((2, topk, tokens), F32),
                pltpu.VMEM((ep * CAP, 2, hidden), F32),
                pltpu.VMEM((width, SUB * 2 * hidden), BF),
                pltpu.VMEM((SUB * hidden, width), BF),
                pltpu.VMEM((ep * CAP, 2, hidden), F32),
                pltpu.VMEM((2, groups, block_rows, width), BF),
                pltpu.VMEM((groups, block_rows, width), BF),
                pltpu.VMEM((groups * block_rows, width), F32),
                pltpu.VMEM((groups * block_rows, width), F32),
                pltpu.VMEM((2, high, PAIR, block_rows, width), BF),
                pltpu.VMEM((high, PAIR, block_rows, hidden), BF),
                pltpu.VMEM((high, PAIR, block_rows, 2 * hidden), BF),
                pltpu.VMEM((ep * block_rows, SUB * 2 * hidden), BF),
                pltpu.VMEM((2, high, block_rows, width), BF),
                pltpu.VMEM((2, high, block_rows, width), F32),
                pltpu.VMEM((2, high, block_rows, width), BF),
                pltpu.VMEM((2, high, block_rows, width), BF),
                pltpu.VMEM((2, high, block_rows, width), BF),
                pltpu.VMEM((2, groups * block_rows, tokens), F32),
                pltpu.VMEM((2, groups * block_rows, tokens), F32),
                pltpu.VMEM((tokens, model), BF),
                pltpu.VMEM((tokens, model), BF),
                pltpu.SemaphoreType.DMA((5 + 5 * SUB,)),
                pltpu.SemaphoreType.DMA((SUB,)),
            ]
            + [pltpu.SemaphoreType.DMA((2, high))] * 4
            + [pltpu.SemaphoreType.DMA((2, cuts))] * 2
            + [pltpu.SemaphoreType.DMA((2, cuts, high))] * 2
            + [pltpu.SemaphoreType.DMA((2,))] * 2
            + [pltpu.SemaphoreType.DMA] * 2
            + [pltpu.SemaphoreType.DMA((2,))] * 2,
            compiler_params=pltpu.CompilerParams(
                collective_id=0, has_side_effects=True, vmem_limit_bytes=VMEM_BYTES
            ),
            name="experts",
        )(
            x[0], dy[0], rf[0].T, rb[0].T, sf[0].T, sb[0].T,
            saved.reshape(ep * CAP, 2, hidden), wg, wu, wd,
        )
        out = pl.pallas_call(
            write_kernel,
            out_shape=jax.ShapeDtypeStruct((tokens, model), BF),
            in_specs=[anywhere],
            out_specs=anywhere,
            scratch_shapes=[
                pltpu.VMEM((SUB, tokens, width), BF),
                pltpu.SemaphoreType.DMA((SUB,)),
                pltpu.SemaphoreType.DMA((SUB,)),
            ],
            compiler_params=pltpu.CompilerParams(vmem_limit_bytes=VMEM_BYTES),
            name="write",
        )(out)
        return out[None]

    in_specs = (
        P("pp", "ep", None),
        P("pp", "ep", None),
        P("pp", "ep", None),
        P("pp", "ep", None),
        P("pp", "ep", None),
        P("pp", "ep", None),
        P("pp", None, None, None, "ep"),
        P(None, "ep"),
        P(None, "ep"),
        P("ep", None),
    )
    out_specs = P("pp", "ep", None)
    return jax.shard_map(body, mesh=mesh, in_specs=in_specs, out_specs=out_specs, check_vma=False)
```
